32 devices in a mesh: seq: 8 (over z, x), head: 4 (over y, core).
Axes of the slice: x: 2, y: 2, z: 4, core: 2. Of those that a mesh axis runs over, the one named last changes fastest.
Arguments:
- block_input: bfloat16 [1, 1024, 1024], P(None, 'seq', 'head'), may hold values from -6 to 6
- norm_gain: float32 [1024], replicated, may hold values from 0.5 to 1.5
- w_query: bfloat16 [1024, 512], P(None, 'head'), may hold values from -0.1875 to 0.1875
- w_key: bfloat16 [1024, 512], P(None, 'head'), may hold values from -0.1875 to 0.1875
- w_value: bfloat16 [1024, 1024], P(None, 'head'), may hold values from -0.1875 to 0.1875
- w_outgate: bfloat16 [1024, 1024], P(None, 'head'), may hold values from -0.1875 to 0.1875
- w_rank: bfloat16 [1024, 16], replicated, may hold values from -0.1875 to 0.1875
- w_expand: bfloat16 [16, 512], P(None, 'head'), may hold values from -1.5 to 1.5
- gate_bias: float32 [512], P('head'), may hold values from 0.3 to 10, as said below
- w_output: bfloat16 [1024, 1024], P('head'), may hold values from -0.1875 to 0.1875
- ffn_gain: float32 [1024], replicated, may hold values from 0.5 to 1.5
- w_gate: bfloat16 [1024, 2816], P(None, 'head'), may hold values from -0.1875 to 0.1875
- w_up: bfloat16 [1024, 2816], P(None, 'head'), may hold values from -0.1875 to 0.1875
- w_down: bfloat16 [2816, 1024], P('head'), may hold values from -0.109375 to 0.109375
- cotangent: bfloat16 [1, 1024, 1024], P(None, 'seq', 'head'), may hold values from -6 to 6
Outputs:
- output: bfloat16 [1, 1024, 1024], P(None, 'seq', 'head')
- grad_input: float32 [1, 1024, 1024], P(None, 'seq', 'head')
- grad_norm_gain: float32 [1024], P('head')
- grad_w_query: float32 [1024, 512], P('seq', 'head')
- grad_w_key: float32 [1024, 512], P('seq', 'head')
- grad_w_value: float32 [1024, 1024], P('seq', 'head')
- grad_w_outgate: float32 [1024, 1024], P('seq', 'head')
- grad_w_rank: float32 [1024, 16], P('seq')
- grad_w_expand: float32 [16, 512], P(None, 'head')
- grad_gate_bias: float32 [512], P('head')
- grad_w_output: float32 [1024, 1024], P('head', 'seq')
- grad_ffn_gain: float32 [1024], P('head')
- grad_w_gate: float32 [1024, 2816], P('seq', 'head')
- grad_w_up: float32 [1024, 2816], P('seq', 'head')
- grad_w_down: float32 [2816, 1024], P('head', 'seq')
The draws below stay inside these ranges and needn't reach their ends.
Inputs may be any that keep to these rules, and one draw needn't show every extreme that they name: `gate_bias`: bias of the forget gate's logits.
All inputs are finite; a program needn't handle non-finite values.
Results may differ from the reference program's by a relative error of at most 0.012.
Values may be sent and summed in bfloat16 or wider, within the bound.
A program may use at most 128 MiB of HBM per device.

```python
import jax
import jax.numpy as jnp
from jax import lax

D = 1024
HEADS = 4
KH = 128
VH = 256
RANK = 16
FF = 2816
GROUP = 64
SEQS = 1
LEN = 1024


def draw_gate_bias(key, part):
    key_spread, key_mode = jax.random.split(key)
    spread = jax.random.uniform(key_spread, (HEADS * KH,), jnp.float32)
    slow_mask = jax.random.uniform(key_mode, (HEADS * KH,), jnp.float32) < 0.5
    low_rate = jnp.where(slow_mask, 0.3 / LEN, 1.5 / LEN).astype(jnp.float32)
    high_rate = jnp.where(slow_mask, 1.5 / LEN, 1.0 / 30.0).astype(jnp.float32)
    forget_rate = jnp.exp(jnp.log(low_rate) + spread * (jnp.log(high_rate) - jnp.log(low_rate)))
    scaled_rate = 16.0 * forget_rate
    return -scaled_rate - jnp.log(-jnp.expm1(-scaled_rate))


def spiked(values, rng, source, target, shards_of, factor):
    owner, partner = [(jnp.arange(values.shape[axis_at]) // (values.shape[axis_at] // shards_of)).reshape([-1 if axis == axis_at else 1 for axis in range(values.ndim)]) for axis_at in (source, target)]
    chosen = jax.random.permutation(rng, shards_of)[partner]
    strong = (owner == chosen) | (owner == (partner + shards_of // 2) % shards_of)
    return jnp.where(strong, factor * values, values)


def block_levels(stream_key, shape, cuts, least, top_value):
    gain, own = 1.0, jax.random.fold_in(stream_key, 6)
    for axis_at, parts in cuts:
        steps = jnp.exp(jax.random.uniform(jax.random.fold_in(own, axis_at), (parts,), jnp.float32, least / len(cuts), top_value / len(cuts)))
        gain = gain * jnp.repeat(steps, shape[axis_at] // parts).reshape([-1 if axis == axis_at else 1 for axis in range(len(shape))])
    return gain


def normal_values(key, dims, deviation, limit, cuts=(), dtype=jnp.bfloat16):
    array = deviation * jax.random.normal(key, dims, jnp.float32)
    if cuts:
        array = array * block_levels(key, dims, cuts, -0.22, 0.18)
    return jnp.clip(array, -limit, limit).astype(dtype)


def bell_draw_with(key, dims, width, limit, cuts, heavy, dtype=jnp.bfloat16):
    array = width * jax.random.normal(key, dims, jnp.float32)
    if cuts:
        array = array * block_levels(key, dims, cuts, -0.22, 0.18)
    return jnp.clip(spiked(array, jax.random.fold_in(key, 3), *heavy), -limit, limit).astype(dtype)


def setup_inputs(seed: int = 0) -> dict:
    key_of = jax.random.split(jax.random.key(seed), 16)
    block_input = bell_draw_with(key_of[0], (SEQS, LEN, D), 1.0, 6.0, ((1, 8), (2, 4)), (1, 2, 8, 2.0))
    norm_gain = jnp.clip(1.0 + 0.1 * jax.random.normal(key_of[1], (D,), jnp.float32), 0.5, 1.5)
    w_query = normal_values(key_of[2], (D, HEADS * KH), D ** -0.5, 0.1875, ((1, 4),))
    w_key = normal_values(key_of[3], (D, HEADS * KH), D ** -0.5, 0.1875, ((1, 4),))
    w_value = normal_values(key_of[4], (D, HEADS * VH), D ** -0.5, 0.1875, ((1, 4),))
    w_outgate = normal_values(key_of[5], (D, HEADS * VH), D ** -0.5, 0.1875, ((1, 4),))
    w_rank = normal_values(key_of[6], (D, RANK), D ** -0.5, 0.1875)
    w_expand = normal_values(key_of[7], (RANK, HEADS * KH), RANK ** -0.5, 1.5, ((1, 4),))
    gate_bias = draw_gate_bias(jax.random.fold_in(key_of[15], 71), 0)
    w_output = normal_values(key_of[9], (HEADS * VH, D), (HEADS * VH) ** -0.5, 0.1875, ((0, 4),))
    ffn_gain = jnp.clip(1.0 + 0.1 * jax.random.normal(key_of[10], (D,), jnp.float32), 0.5, 1.5)
    w_gate = normal_values(key_of[11], (D, FF), D ** -0.5, 0.1875, ((1, 4),))
    w_up = normal_values(key_of[12], (D, FF), D ** -0.5, 0.1875, ((1, 4),))
    w_down = normal_values(key_of[13], (FF, D), FF ** -0.5, 0.109375, ((0, 4),))
    cotangent = bell_draw_with(key_of[14], (SEQS, LEN, D), 1.0, 6.0, ((1, 8), (2, 4)), (1, 2, 8, 2.0))
    return dict(block_input=block_input, norm_gain=norm_gain, w_query=w_query, w_key=w_key, w_value=w_value, w_outgate=w_outgate, w_rank=w_rank, w_expand=w_expand, gate_bias=gate_bias, w_output=w_output, ffn_gain=ffn_gain, w_gate=w_gate, w_up=w_up, w_down=w_down, cotangent=cotangent)


EPS = 1e-06
HEAD_EPS = 1e-05
PRECISE = lax.Precision.HIGHEST

@jax.custom_vjp
def low(v):
    return lax.optimization_barrier(v.astype(jnp.bfloat16)).astype(jnp.float32)

@jax.custom_vjp
def low_back(v):
    return v

def low_keep(v):
    return (low(v), None)

def low_pass(kept, grad):
    return (grad,)

def back_keep(v):
    return (v, None)

def back_low(kept, grad):
    return (low(grad),)
low.defvjp(low_keep, low_pass)
low_back.defvjp(back_keep, back_low)

def matmul_high(left_side, right_side):
    return jnp.dot(left_side, right_side, precision=PRECISE)

def rms_norm(values_in, epsilon):
    return values_in * lax.rsqrt(lax.optimization_barrier(jnp.mean(values_in * values_in, axis=-1, keepdims=True)) + epsilon)

def group_step(carry_state, block_inputs):
    q_block, k_block, v_block, g_block = block_inputs
    block_len = q_block.shape[0]
    cumulative = jnp.cumsum(g_block, axis=0)
    final_sum = cumulative[-1]
    q_decay = q_block * jnp.exp(cumulative)
    k_decay = k_block * jnp.exp(-cumulative)
    scores = matmul_high(q_decay, k_decay.T)
    row_index = lax.broadcasted_iota(jnp.int32, (block_len, block_len), 0)
    col_index = lax.broadcasted_iota(jnp.int32, (block_len, block_len), 1)
    scores = jnp.where(row_index >= col_index, scores, jnp.zeros_like(scores))
    block_out = matmul_high(q_decay, carry_state) + matmul_high(scores, v_block)
    k_tail = k_block * jnp.exp(final_sum - cumulative)
    carry_state = jnp.exp(final_sum)[:, None] * carry_state + matmul_high(k_tail.T, v_block)
    return (carry_state, block_out)

def run_sequence(q_seq, k_seq, v_seq, g_seq):
    blocks = q_seq.shape[0] // GROUP

    def to_blocks(tensor):
        return tensor.reshape(blocks, GROUP, tensor.shape[-1])
    start_state = jnp.zeros((q_seq.shape[-1], v_seq.shape[-1]), jnp.float32)
    end_state, block_outs = lax.scan(jax.checkpoint(group_step), start_state, (to_blocks(q_seq), to_blocks(k_seq), to_blocks(v_seq), to_blocks(g_seq)))
    return block_outs.reshape(q_seq.shape[0], v_seq.shape[-1])

def heads_of(tensor, head_width):
    return tensor.reshape(tensor.shape[0], HEADS, head_width).transpose(1, 0, 2)

def forward(block_input, norm_gain, w_query, w_key, w_value, w_outgate, w_rank, w_expand, gate_bias, w_output, ffn_gain, w_gate, w_up, w_down):
    normed = low(rms_norm(block_input, EPS) * norm_gain)
    query = low_back(matmul_high(normed, w_query)) * KH ** (-0.5)
    key_proj = low_back(matmul_high(normed, w_key))
    value_proj = low_back(matmul_high(normed, w_value))
    outgate = low_back(matmul_high(normed, w_outgate))
    lowrank = matmul_high(normed, w_rank)
    logdecay = jax.nn.log_sigmoid(matmul_high(lowrank, w_expand) + gate_bias) / 16.0
    mixed = jax.vmap(run_sequence)(heads_of(query, KH), heads_of(key_proj, KH), heads_of(value_proj, VH), heads_of(logdecay, KH))
    mixed = mixed.transpose(1, 0, 2)
    head_norm = rms_norm(mixed, HEAD_EPS)
    gated = head_norm * jax.nn.silu(outgate.reshape(-1, HEADS, VH))
    branch = low(gated.reshape(-1, HEADS * VH))
    middle = block_input + low_back(matmul_high(branch, w_output))
    normed_two = low(rms_norm(low(middle), EPS) * ffn_gain)
    gate = low_back(matmul_high(normed_two, w_gate))
    up_proj = low_back(matmul_high(normed_two, w_up))
    hidden = low(jax.nn.silu(gate) * up_proj)
    return middle + matmul_high(hidden, w_down)

def reference(block_input, norm_gain, w_query, w_key, w_value, w_outgate, w_rank, w_expand, gate_bias, w_output, ffn_gain, w_gate, w_up, w_down, cotangent):
    weights = tuple((w.astype(jnp.float32) for w in (norm_gain, w_query, w_key, w_value, w_outgate, w_rank, w_expand, gate_bias, w_output, ffn_gain, w_gate, w_up, w_down)))

    def one_sequence(totals, seq_pair):
        seq_input, seq_cot = seq_pair
        result, pullback = jax.vjp(forward, seq_input.astype(jnp.float32), *weights)
        gradients = pullback(seq_cot.astype(jnp.float32))
        totals = tuple((running + gradient for running, gradient in zip(totals, gradients[1:])))
        return (totals, (result.astype(jnp.bfloat16), gradients[0]))
    start = tuple((jnp.zeros_like(w) for w in weights))
    sums, (outputs, grad_inputs) = lax.scan(one_sequence, start, (block_input, cotangent))
    return (outputs, grad_inputs, sums[0], sums[1], sums[2], sums[3], sums[4], sums[5], sums[6], sums[7], sums[8], sums[9], sums[10], sums[11], sums[12])
```

```python
import jax
import jax.numpy as jnp
from jax import lax
from jax.sharding import PartitionSpec as P

GROUP = 64


EPS = 1e-06
HEAD_EPS = 1e-05
PRECISE = lax.Precision.HIGHEST


def carried_in(shard, axis, combine, identity, reverse):
    peers, here = (lax.axis_size(axis), lax.axis_index(axis))
    everything = jax.tree.map(lambda part: lax.all_gather(part, axis), shard)
    start = jax.tree.map(
        lambda part, zero: jnp.broadcast_to(jnp.asarray(zero, part.dtype), part.shape),
        shard,
        identity,
    )

    def turn(k, before):
        at = peers - 1 - k if reverse else k
        reached = at > here if reverse else at < here
        new = combine(before, jax.tree.map(lambda part: part[at], everything))
        return jax.tree.map(lambda a, b: jnp.where(reached, a, b), new, before)

    return lax.fori_loop(0, peers, turn, start)


def matmul_high(left_side, right_side):
    return jnp.dot(left_side, right_side, precision=PRECISE)


def rows_product(left_side, right_side):
    return lax.dot_general(
        left_side, right_side, (((0,), (0,)), ((), ())), preferred_element_type=jnp.float32
    )


def cross_product(left_side, right_side):
    return lax.dot_general(
        left_side, right_side, (((1,), (1,)), ((), ())), preferred_element_type=jnp.float32
    )


def running_sum(tensor):
    length = tensor.shape[0]
    row_index = lax.broadcasted_iota(jnp.int32, (length, length), 0)
    col_index = lax.broadcasted_iota(jnp.int32, (length, length), 1)
    return matmul_high((row_index >= col_index).astype(jnp.float32), tensor)


def group_step(carry_state, block_inputs):
    q_block, k_block, v_block, g_block = block_inputs
    block_len = q_block.shape[0]
    cumulative = running_sum(g_block)
    final_sum = cumulative[-1]
    q_decay = q_block * jnp.exp(cumulative)
    k_decay = k_block * jnp.exp(-cumulative)
    scores = matmul_high(q_decay, k_decay.T)
    row_index = lax.broadcasted_iota(jnp.int32, (block_len, block_len), 0)
    col_index = lax.broadcasted_iota(jnp.int32, (block_len, block_len), 1)
    scores = jnp.where(row_index >= col_index, scores, jnp.zeros_like(scores))
    block_out = matmul_high(q_decay, carry_state) + matmul_high(scores, v_block)
    k_tail = k_block * jnp.exp(final_sum - cumulative)
    carry_state = jnp.exp(final_sum)[:, None] * carry_state + matmul_high(k_tail.T, v_block)
    return (carry_state, block_out)


def span_run(q_seq, k_seq, v_seq, g_seq, start_state):
    blocks = q_seq.shape[0] // GROUP

    def to_blocks(tensor):
        return tensor.reshape(blocks, GROUP, tensor.shape[-1])

    end_state, block_outs = lax.scan(
        jax.checkpoint(group_step),
        start_state,
        (to_blocks(q_seq), to_blocks(k_seq), to_blocks(v_seq), to_blocks(g_seq)),
    )
    return (block_outs.reshape(q_seq.shape[0], v_seq.shape[-1]), end_state)


def run_all(q_all, k_all, v_all, g_all, start_all):
    return jax.vmap(span_run)(q_all, k_all, v_all, g_all, start_all)


def combine(earlier, later):
    return (earlier[0] + later[0], jnp.exp(later[0])[:, :, None] * earlier[1] + later[1])


def body(
    block_input,
    norm_gain,
    w_query,
    w_key,
    w_value,
    w_outgate,
    w_rank,
    w_expand,
    gate_bias,
    w_output,
    ffn_gain,
    w_gate,
    w_up,
    w_down,
    cotangent,
):
    seq_count, span_len, part_width = block_input.shape
    row_count = seq_count * span_len
    head_count = lax.axis_size("head")
    full_width = part_width * head_count
    col_start = lax.axis_index("head") * part_width
    key_width = w_query.shape[1]
    value_width = w_value.shape[1]
    query_scale = key_width ** (-0.5)

    def per_seq(tensor):
        return tensor.reshape(seq_count, span_len, tensor.shape[-1])

    def mine(tensor):
        return lax.dynamic_slice_in_dim(tensor, col_start, part_width, tensor.ndim - 1)

    input_part = block_input.reshape(row_count, part_width)
    input_rows = lax.all_gather(input_part, "head", axis=1, tiled=True)
    input_wide = input_rows.astype(jnp.float32)
    inverse_one = lax.rsqrt(jnp.mean(input_wide * input_wide, axis=1, keepdims=True) + EPS)
    normal_one = input_wide * inverse_one
    normed = (normal_one * norm_gain).astype(jnp.bfloat16)
    query_proj = jnp.dot(normed, w_query, preferred_element_type=jnp.float32)
    key_proj = jnp.dot(normed, w_key, preferred_element_type=jnp.float32)
    value_proj = jnp.dot(normed, w_value, preferred_element_type=jnp.float32)
    outgate = jnp.dot(normed, w_outgate, preferred_element_type=jnp.float32)
    lowrank = jnp.dot(normed, w_rank, preferred_element_type=jnp.float32)
    expand_wide = w_expand.astype(jnp.float32)
    preact = matmul_high(lowrank, expand_wide) + gate_bias
    logdecay = jax.nn.log_sigmoid(preact) / 16.0
    q_seq = per_seq(query_proj) * query_scale
    k_seq = per_seq(key_proj)
    v_seq = per_seq(value_proj)
    g_seq = per_seq(logdecay)
    zero_state = jnp.zeros((seq_count, key_width, value_width), jnp.float32)
    local_out, local_state = run_all(q_seq, k_seq, v_seq, g_seq, zero_state)
    cumulative = jax.vmap(running_sum)(g_seq)
    carry_query = q_seq * jnp.exp(cumulative)
    decay_total = cumulative[:, -1, :]
    identity = (jnp.zeros_like(decay_total), zero_state)
    scanned = carried_in((decay_total, local_state), "seq", combine, identity, False)
    entering = scanned[1]
    mixer_out = local_out + jnp.einsum("sti,siv->stv", carry_query, entering, precision=PRECISE)
    mixer_out = mixer_out.reshape(row_count, value_width)
    head_inv = lax.rsqrt(jnp.mean(mixer_out * mixer_out, axis=1, keepdims=True) + HEAD_EPS)
    head_norm = mixer_out * head_inv
    outgate_sig = jax.nn.sigmoid(outgate)
    swish_gate = outgate * outgate_sig
    branch = (head_norm * swish_gate).astype(jnp.bfloat16)
    attn_part = jnp.dot(branch, w_output, preferred_element_type=jnp.float32)
    attn_mine = lax.psum_scatter(attn_part, "head", scatter_dimension=1, tiled=True)
    middle_part = input_part.astype(jnp.float32) + attn_mine
    middle_low = lax.all_gather(middle_part.astype(jnp.bfloat16), "head", axis=1, tiled=True)
    middle_wide = middle_low.astype(jnp.float32)
    inverse_two = lax.rsqrt(jnp.mean(middle_wide * middle_wide, axis=1, keepdims=True) + EPS)
    normal_two = middle_wide * inverse_two
    normed_two = (normal_two * ffn_gain).astype(jnp.bfloat16)
    gate_pre = jnp.dot(normed_two, w_gate, preferred_element_type=jnp.float32)
    up_pre = jnp.dot(normed_two, w_up, preferred_element_type=jnp.float32)
    gate_sig = jax.nn.sigmoid(gate_pre)
    hidden = (gate_pre * gate_sig * up_pre).astype(jnp.bfloat16)
    ffn_part = jnp.dot(hidden, w_down, preferred_element_type=jnp.float32)
    ffn_mine = lax.psum_scatter(
        ffn_part.astype(jnp.bfloat16), "head", scatter_dimension=1, tiled=True
    ).astype(jnp.float32)
    output = (middle_part + ffn_mine).astype(jnp.bfloat16).reshape(seq_count, span_len, part_width)
    grad_part = cotangent.reshape(row_count, part_width)
    grad_rows = lax.all_gather(grad_part, "head", axis=1, tiled=True)
    grad_hidden = cross_product(grad_rows, w_down)
    grad_gate = (grad_hidden * up_pre * gate_sig * (1.0 + gate_pre * (1.0 - gate_sig))).astype(
        jnp.bfloat16
    )
    grad_upper = (grad_hidden * gate_pre * gate_sig).astype(jnp.bfloat16)
    grad_normed_two = cross_product(grad_gate, w_gate) + cross_product(grad_upper, w_up)
    stat_part = jnp.sum(grad_normed_two * ffn_gain * normal_two, axis=1, keepdims=True)
    grad_two, stat_two = (
        lax.psum_scatter(grad_normed_two, "head", scatter_dimension=1, tiled=True),
        lax.psum_scatter(
            jnp.tile(stat_part, (1, head_count)), "head", scatter_dimension=1, tiled=True
        ),
    )
    normal_mine = mine(normal_two)
    grad_middle = grad_part.astype(jnp.float32) + inverse_two * (
        grad_two * mine(ffn_gain) - normal_mine * stat_two / full_width
    )
    gain_two = jnp.sum(grad_two * normal_mine, axis=0)
    grad_branch_rows = lax.all_gather(grad_middle.astype(jnp.bfloat16), "head", axis=1, tiled=True)
    grad_branch = cross_product(grad_branch_rows, w_output)
    grad_head = grad_branch * swish_gate
    grad_outgate = (
        grad_branch * head_norm * outgate_sig * (1.0 + outgate * (1.0 - outgate_sig))
    ).astype(jnp.bfloat16)
    grad_mixed = head_inv * (
        grad_head - head_norm * jnp.mean(grad_head * head_norm, axis=1, keepdims=True)
    )
    grad_seq = per_seq(grad_mixed)
    state_pull = jnp.einsum("sti,stv->siv", carry_query, grad_seq, precision=PRECISE)
    later = carried_in((decay_total, state_pull), "seq", combine, identity, True)
    later_grad = later[1]
    _, back_fn = jax.vjp(run_all, q_seq, k_seq, v_seq, g_seq, entering)
    grad_qseq, grad_kseq, grad_vseq, grad_gseq, _ = back_fn((grad_seq, later_grad))
    grad_query = (grad_qseq.reshape(row_count, key_width) * query_scale).astype(jnp.bfloat16)
    grad_keys = grad_kseq.reshape(row_count, key_width).astype(jnp.bfloat16)
    grad_values = grad_vseq.reshape(row_count, value_width).astype(jnp.bfloat16)
    grad_pre = grad_gseq.reshape(row_count, key_width) / 16.0 * jax.nn.sigmoid(-preact)
    grad_expand = lax.dot_general(lowrank, grad_pre, (((0,), (0,)), ((), ())), precision=PRECISE)
    grad_bias = jnp.sum(grad_pre, axis=0)
    grad_lowrank = lax.dot_general(
        grad_pre, expand_wide, (((1,), (1,)), ((), ())), precision=PRECISE
    )
    rank_wide = w_rank.astype(jnp.float32)
    grad_normed = (
        cross_product(grad_query, w_query)
        + cross_product(grad_keys, w_key)
        + cross_product(grad_values, w_value)
        + cross_product(grad_outgate, w_outgate)
        + lax.dot_general(grad_lowrank, rank_wide, (((1,), (1,)), ((), ())), precision=PRECISE)
    )
    stat_one_part = jnp.sum(grad_normed * norm_gain * normal_one, axis=1, keepdims=True)
    grad_one, stat_one, lowrank_total = (
        lax.psum_scatter(
            grad_normed.astype(jnp.bfloat16), "head", scatter_dimension=1, tiled=True
        ).astype(jnp.float32),
        lax.psum_scatter(
            jnp.tile(stat_one_part, (1, head_count)).astype(jnp.bfloat16),
            "head",
            scatter_dimension=1,
            tiled=True,
        ).astype(jnp.float32),
        lax.psum_scatter(
            jnp.tile(grad_lowrank, (1, head_count)).astype(jnp.bfloat16),
            "head",
            scatter_dimension=1,
            tiled=True,
        ).astype(jnp.float32),
    )
    normal_one_mine = mine(normal_one)
    grad_inputs = grad_middle + inverse_one * (
        grad_one * mine(norm_gain) - normal_one_mine * stat_one / full_width
    )
    gain_one = jnp.sum(grad_one * normal_one_mine, axis=0)
    def columns_of_all(tensor):
        return lax.all_to_all(tensor, "seq", split_axis=1, concat_axis=0, tiled=True)

    def tokens_of_all(tensor):
        return lax.all_gather(tensor, "seq", axis=0, tiled=True)

    columns_one = columns_of_all(normed)
    columns_two = columns_of_all(normed_two)
    columns_cot = columns_of_all(grad_rows)
    columns_branch = columns_of_all(grad_branch_rows)
    mixer_all = tokens_of_all(
        jnp.concatenate([grad_query, grad_keys, grad_values, grad_outgate], axis=1)
    )
    mixer_sum = rows_product(columns_one, mixer_all)
    wide = key_width
    grad_wout = rows_product(tokens_of_all(branch), columns_branch)
    grad_wgate = rows_product(columns_two, tokens_of_all(grad_gate))
    grad_wup = rows_product(columns_two, tokens_of_all(grad_upper))
    grad_wdown = rows_product(tokens_of_all(hidden), columns_cot)
    grad_wrank = rows_product(columns_one, tokens_of_all(lowrank_total.astype(jnp.bfloat16)))
    summed = (
        mixer_sum[:, :wide],
        mixer_sum[:, wide : 2 * wide],
        mixer_sum[:, 2 * wide : 2 * wide + value_width],
        mixer_sum[:, 2 * wide + value_width :],
        grad_wrank,
        grad_wout,
        grad_wgate,
        grad_wup,
        grad_wdown,
    )
    smalls = lax.psum((grad_expand, grad_bias, gain_one, gain_two), "seq")
    return (
        output,
        grad_inputs.reshape(seq_count, span_len, part_width),
        smalls[2],
        summed[0],
        summed[1],
        summed[2],
        summed[3],
        summed[4],
        smalls[0],
        smalls[1],
        summed[5],
        smalls[3],
        summed[6],
        summed[7],
        summed[8],
    )


def solution(mesh):
    in_specs = (
        P(None, "seq", "head"),
        P(),
        P(None, "head"),
        P(None, "head"),
        P(None, "head"),
        P(None, "head"),
        P(),
        P(None, "head"),
        P("head"),
        P("head", None),
        P(),
        P(None, "head"),
        P(None, "head"),
        P("head", None),
        P(None, "seq", "head"),
    )
    out_specs = (
        P(None, "seq", "head"),
        P(None, "seq", "head"),
        P("head"),
        P("seq", "head"),
        P("seq", "head"),
        P("seq", "head"),
        P("seq", "head"),
        P("seq", None),
        P(None, "head"),
        P("head"),
        P("head", "seq"),
        P("head"),
        P("seq", "head"),
        P("seq", "head"),
        P("head", "seq"),
    )
    return jax.shard_map(body, mesh=mesh, in_specs=in_specs, out_specs=out_specs, check_vma=False)
```

```python
import functools

import jax
import jax.numpy as jnp
from jax import lax
from jax.experimental import pallas as pl
from jax.experimental.pallas import tpu as pltpu
from jax.sharding import PartitionSpec as P

MESH = pl.DeviceIdType.MESH

GROUP = 64


EPS = 1e-06
HEAD_EPS = 1e-05
PRECISE = lax.Precision.HIGHEST


def carried_in(shard, axis, combine, identity, reverse):
    peers, here = (lax.axis_size(axis), lax.axis_index(axis))
    everything = jax.tree.map(lambda part: lax.all_gather(part, axis), shard)
    start = jax.tree.map(
        lambda part, zero: jnp.broadcast_to(jnp.asarray(zero, part.dtype), part.shape),
        shard,
        identity,
    )

    def turn(k, before):
        at = peers - 1 - k if reverse else k
        reached = at > here if reverse else at < here
        new = combine(before, jax.tree.map(lambda part: part[at], everything))
        return jax.tree.map(lambda a, b: jnp.where(reached, a, b), new, before)

    return lax.fori_loop(0, peers, turn, start)


def matmul_high(left_side, right_side):
    return jnp.dot(left_side, right_side, precision=PRECISE)


def rows_product(left_side, right_side):
    return lax.dot_general(
        left_side, right_side, (((0,), (0,)), ((), ())), preferred_element_type=jnp.float32
    )


def cross_product(left_side, right_side):
    return lax.dot_general(
        left_side, right_side, (((1,), (1,)), ((), ())), preferred_element_type=jnp.float32
    )


def running_sum(tensor):
    length = tensor.shape[0]
    row_index = lax.broadcasted_iota(jnp.int32, (length, length), 0)
    col_index = lax.broadcasted_iota(jnp.int32, (length, length), 1)
    return matmul_high((row_index >= col_index).astype(jnp.float32), tensor)


def group_step(carry_state, block_inputs):
    q_block, k_block, v_block, g_block = block_inputs
    block_len = q_block.shape[0]
    cumulative = running_sum(g_block)
    final_sum = cumulative[-1]
    q_decay = q_block * jnp.exp(cumulative)
    k_decay = k_block * jnp.exp(-cumulative)
    scores = matmul_high(q_decay, k_decay.T)
    row_index = lax.broadcasted_iota(jnp.int32, (block_len, block_len), 0)
    col_index = lax.broadcasted_iota(jnp.int32, (block_len, block_len), 1)
    scores = jnp.where(row_index >= col_index, scores, jnp.zeros_like(scores))
    block_out = matmul_high(q_decay, carry_state) + matmul_high(scores, v_block)
    k_tail = k_block * jnp.exp(final_sum - cumulative)
    carry_state = jnp.exp(final_sum)[:, None] * carry_state + matmul_high(k_tail.T, v_block)
    return (carry_state, block_out)


def span_run(q_seq, k_seq, v_seq, g_seq, start_state):
    blocks = q_seq.shape[0] // GROUP

    def to_blocks(tensor):
        return tensor.reshape(blocks, GROUP, tensor.shape[-1])

    end_state, block_outs = lax.scan(
        jax.checkpoint(group_step),
        start_state,
        (to_blocks(q_seq), to_blocks(k_seq), to_blocks(v_seq), to_blocks(g_seq)),
    )
    return (block_outs.reshape(q_seq.shape[0], v_seq.shape[-1]), end_state)


def run_all(q_all, k_all, v_all, g_all, start_all):
    return jax.vmap(span_run)(q_all, k_all, v_all, g_all, start_all)


def combine(earlier, later):
    return (earlier[0] + later[0], jnp.exp(later[0])[:, :, None] * earlier[1] + later[1])


def body(
    block_input,
    norm_gain,
    w_query,
    w_key,
    w_value,
    w_outgate,
    w_rank,
    w_expand,
    gate_bias,
    w_output,
    ffn_gain,
    w_gate,
    w_up,
    w_down,
    cotangent,
):
    seq_count, span_len, part_width = block_input.shape
    row_count = seq_count * span_len
    head_count = lax.axis_size("head")
    full_width = part_width * head_count
    col_start = lax.axis_index("head") * part_width
    key_width = w_query.shape[1]
    value_width = w_value.shape[1]
    query_scale = key_width ** (-0.5)

    def per_seq(tensor):
        return tensor.reshape(seq_count, span_len, tensor.shape[-1])

    def mine(tensor):
        return lax.dynamic_slice_in_dim(tensor, col_start, part_width, tensor.ndim - 1)

    input_part = block_input.reshape(row_count, part_width)
    input_rows = lax.all_gather(input_part, "head", axis=1, tiled=True)
    input_wide = input_rows.astype(jnp.float32)
    inverse_one = lax.rsqrt(jnp.mean(input_wide * input_wide, axis=1, keepdims=True) + EPS)
    normal_one = input_wide * inverse_one
    normed = (normal_one * norm_gain).astype(jnp.bfloat16)
    query_proj = jnp.dot(normed, w_query, preferred_element_type=jnp.float32)
    key_proj = jnp.dot(normed, w_key, preferred_element_type=jnp.float32)
    value_proj = jnp.dot(normed, w_value, preferred_element_type=jnp.float32)
    outgate = jnp.dot(normed, w_outgate, preferred_element_type=jnp.float32)
    lowrank = jnp.dot(normed, w_rank, preferred_element_type=jnp.float32)
    expand_wide = w_expand.astype(jnp.float32)
    preact = matmul_high(lowrank, expand_wide) + gate_bias
    logdecay = jax.nn.log_sigmoid(preact) / 16.0
    q_seq = per_seq(query_proj) * query_scale
    k_seq = per_seq(key_proj)
    v_seq = per_seq(value_proj)
    g_seq = per_seq(logdecay)
    zero_state = jnp.zeros((seq_count, key_width, value_width), jnp.float32)
    local_out, local_state = run_all(q_seq, k_seq, v_seq, g_seq, zero_state)
    cumulative = jax.vmap(running_sum)(g_seq)
    carry_query = q_seq * jnp.exp(cumulative)
    decay_total = cumulative[:, -1, :]
    identity = (jnp.zeros_like(decay_total), zero_state)
    scanned = carried_in((decay_total, local_state), "seq", combine, identity, False)
    entering = scanned[1]
    mixer_out = local_out + jnp.einsum("sti,siv->stv", carry_query, entering, precision=PRECISE)
    mixer_out = mixer_out.reshape(row_count, value_width)
    head_inv = lax.rsqrt(jnp.mean(mixer_out * mixer_out, axis=1, keepdims=True) + HEAD_EPS)
    head_norm = mixer_out * head_inv
    outgate_sig = jax.nn.sigmoid(outgate)
    swish_gate = outgate * outgate_sig
    branch = (head_norm * swish_gate).astype(jnp.bfloat16)
    attn_part = jnp.dot(branch, w_output, preferred_element_type=jnp.float32)
    attn_mine = lax.psum_scatter(attn_part, "head", scatter_dimension=1, tiled=True)
    middle_part = input_part.astype(jnp.float32) + attn_mine
    middle_low = lax.all_gather(middle_part.astype(jnp.bfloat16), "head", axis=1, tiled=True)
    middle_wide = middle_low.astype(jnp.float32)
    inverse_two = lax.rsqrt(jnp.mean(middle_wide * middle_wide, axis=1, keepdims=True) + EPS)
    normal_two = middle_wide * inverse_two
    normed_two = (normal_two * ffn_gain).astype(jnp.bfloat16)
    gate_pre = jnp.dot(normed_two, w_gate, preferred_element_type=jnp.float32)
    up_pre = jnp.dot(normed_two, w_up, preferred_element_type=jnp.float32)
    gate_sig = jax.nn.sigmoid(gate_pre)
    hidden = (gate_pre * gate_sig * up_pre).astype(jnp.bfloat16)
    ffn_part = jnp.dot(hidden, w_down, preferred_element_type=jnp.float32)
    ffn_mine = lax.psum_scatter(
        ffn_part.astype(jnp.bfloat16), "head", scatter_dimension=1, tiled=True
    ).astype(jnp.float32)
    output = (middle_part + ffn_mine).astype(jnp.bfloat16).reshape(seq_count, span_len, part_width)
    grad_part = cotangent.reshape(row_count, part_width)
    grad_rows = lax.all_gather(grad_part, "head", axis=1, tiled=True)
    grad_hidden = cross_product(grad_rows, w_down)
    grad_gate = (grad_hidden * up_pre * gate_sig * (1.0 + gate_pre * (1.0 - gate_sig))).astype(
        jnp.bfloat16
    )
    grad_upper = (grad_hidden * gate_pre * gate_sig).astype(jnp.bfloat16)
    grad_normed_two = cross_product(grad_gate, w_gate) + cross_product(grad_upper, w_up)
    stat_part = jnp.sum(grad_normed_two * ffn_gain * normal_two, axis=1, keepdims=True)
    grad_two, stat_two = (
        lax.psum_scatter(grad_normed_two, "head", scatter_dimension=1, tiled=True),
        lax.psum_scatter(
            jnp.tile(stat_part, (1, head_count)), "head", scatter_dimension=1, tiled=True
        ),
    )
    normal_mine = mine(normal_two)
    grad_middle = grad_part.astype(jnp.float32) + inverse_two * (
        grad_two * mine(ffn_gain) - normal_mine * stat_two / full_width
    )
    gain_two = jnp.sum(grad_two * normal_mine, axis=0)
    grad_branch_rows = lax.all_gather(grad_middle.astype(jnp.bfloat16), "head", axis=1, tiled=True)
    grad_branch = cross_product(grad_branch_rows, w_output)
    grad_head = grad_branch * swish_gate
    grad_outgate = (
        grad_branch * head_norm * outgate_sig * (1.0 + outgate * (1.0 - outgate_sig))
    ).astype(jnp.bfloat16)
    grad_mixed = head_inv * (
        grad_head - head_norm * jnp.mean(grad_head * head_norm, axis=1, keepdims=True)
    )
    grad_seq = per_seq(grad_mixed)
    state_pull = jnp.einsum("sti,stv->siv", carry_query, grad_seq, precision=PRECISE)
    later = carried_in((decay_total, state_pull), "seq", combine, identity, True)
    later_grad = later[1]
    _, back_fn = jax.vjp(run_all, q_seq, k_seq, v_seq, g_seq, entering)
    grad_qseq, grad_kseq, grad_vseq, grad_gseq, _ = back_fn((grad_seq, later_grad))
    grad_query = (grad_qseq.reshape(row_count, key_width) * query_scale).astype(jnp.bfloat16)
    grad_keys = grad_kseq.reshape(row_count, key_width).astype(jnp.bfloat16)
    grad_values = grad_vseq.reshape(row_count, value_width).astype(jnp.bfloat16)
    grad_pre = grad_gseq.reshape(row_count, key_width) / 16.0 * jax.nn.sigmoid(-preact)
    grad_expand = lax.dot_general(lowrank, grad_pre, (((0,), (0,)), ((), ())), precision=PRECISE)
    grad_bias = jnp.sum(grad_pre, axis=0)
    grad_lowrank = lax.dot_general(
        grad_pre, expand_wide, (((1,), (1,)), ((), ())), precision=PRECISE
    )
    rank_wide = w_rank.astype(jnp.float32)
    grad_normed = (
        cross_product(grad_query, w_query)
        + cross_product(grad_keys, w_key)
        + cross_product(grad_values, w_value)
        + cross_product(grad_outgate, w_outgate)
        + lax.dot_general(grad_lowrank, rank_wide, (((1,), (1,)), ((), ())), precision=PRECISE)
    )
    stat_one_part = jnp.sum(grad_normed * norm_gain * normal_one, axis=1, keepdims=True)
    grad_one, stat_one, lowrank_total = (
        lax.psum_scatter(
            grad_normed.astype(jnp.bfloat16), "head", scatter_dimension=1, tiled=True
        ).astype(jnp.float32),
        lax.psum_scatter(
            jnp.tile(stat_one_part, (1, head_count)).astype(jnp.bfloat16),
            "head",
            scatter_dimension=1,
            tiled=True,
        ).astype(jnp.float32),
        lax.psum_scatter(
            jnp.tile(grad_lowrank, (1, head_count)).astype(jnp.bfloat16),
            "head",
            scatter_dimension=1,
            tiled=True,
        ).astype(jnp.float32),
    )
    normal_one_mine = mine(normal_one)
    grad_inputs = grad_middle + inverse_one * (
        grad_one * mine(norm_gain) - normal_one_mine * stat_one / full_width
    )
    gain_one = jnp.sum(grad_one * normal_one_mine, axis=0)
    def columns_of_all(tensor):
        return lax.all_to_all(tensor, "seq", split_axis=1, concat_axis=0, tiled=True)

    def tokens_of_all(tensor):
        return lax.all_gather(tensor, "seq", axis=0, tiled=True)

    columns_one = columns_of_all(normed)
    columns_two = columns_of_all(normed_two)
    columns_cot = columns_of_all(grad_rows)
    columns_branch = columns_of_all(grad_branch_rows)
    mixer_all = tokens_of_all(
        jnp.concatenate([grad_query, grad_keys, grad_values, grad_outgate], axis=1)
    )
    mixer_sum = rows_product(columns_one, mixer_all)
    wide = key_width
    grad_wout = rows_product(tokens_of_all(branch), columns_branch)
    grad_wgate = rows_product(columns_two, tokens_of_all(grad_gate))
    grad_wup = rows_product(columns_two, tokens_of_all(grad_upper))
    grad_wdown = rows_product(tokens_of_all(hidden), columns_cot)
    grad_wrank = rows_product(columns_one, tokens_of_all(lowrank_total.astype(jnp.bfloat16)))
    summed = (
        mixer_sum[:, :wide],
        mixer_sum[:, wide : 2 * wide],
        mixer_sum[:, 2 * wide : 2 * wide + value_width],
        mixer_sum[:, 2 * wide + value_width :],
        grad_wrank,
        grad_wout,
        grad_wgate,
        grad_wup,
        grad_wdown,
    )
    smalls = lax.psum((grad_expand, grad_bias, gain_one, gain_two), "seq")
    return (
        output,
        grad_inputs.reshape(seq_count, span_len, part_width),
        smalls[2],
        summed[0],
        summed[1],
        summed[2],
        summed[3],
        summed[4],
        smalls[0],
        smalls[1],
        summed[5],
        smalls[3],
        summed[6],
        summed[7],
        summed[8],
    )


def dot_nn(a, b):
    return lax.dot_general(a, b, (((1,), (0,)), ((), ())), preferred_element_type=jnp.float32)


def fine(a, b, left, right):
    return lax.dot_general(
        a,
        b,
        (((left,), (right,)), ((), ())),
        precision=PRECISE,
        preferred_element_type=jnp.float32,
    )


def column_of(row):
    size = row.shape[1]
    r = lax.broadcasted_iota(jnp.int32, (size, size), 0)
    c = lax.broadcasted_iota(jnp.int32, (size, size), 1)
    return jnp.sum(jnp.where(r == c, jnp.broadcast_to(row, (size, size)), 0.0), 1, keepdims=True)


HEAD_PHASES = 8
SEQ_PHASES = 9


def whole_kernel(S, H, *refs):
    (x_ref, ng_ref, wq_ref, wk_ref, wv_ref, wog_ref, wr_ref, we_ref, gb_ref, wo_ref, fg_ref,
     wg_ref, wu_ref, wd_ref, cot_ref) = refs[:15]
    (out_ref, gin_ref, gng_ref, gwq_ref, gwk_ref, gwv_ref, gwog_ref, gwr_ref, gwe_ref, gbias_ref,
     gwo_ref, gfg_ref, gwg_ref, gwu_ref, gwd_ref) = refs[15:30]
    (xc, rs_a, rr_a, mid, rs_b, rr_b, rs_c, rr_c, st_two, gbuf, rs_d, rr_d, st_one,
     dts, stf, stb, e_ref, g_ref, cs_a, cr_a, cs_b, cr_b, hid, ggu, act, fsm,
     send_h, recv_h, send_s, recv_s) = refs[30:]
    f32, bf16 = jnp.float32, jnp.bfloat16
    s, h = lax.axis_index("seq"), lax.axis_index("head")
    rows, pw = x_ref.shape
    full = pw * H
    cb = full // S
    kw, vw = wq_ref.shape[1], wv_ref.shape[1]
    blocks = rows // GROUP
    scale = kw ** (-0.5)
    pending = []

    barrier = pltpu.get_barrier_semaphore()
    for j in range(1, H):
        pl.semaphore_signal(barrier, inc=1, device_id={"head": lax.rem(h + j, H)}, device_id_type=MESH)
    for j in range(1, S):
        pl.semaphore_signal(barrier, inc=1, device_id={"seq": lax.rem(s + j, S)}, device_id_type=MESH)
    pl.semaphore_wait(barrier, H + S - 2)

    def head_send(phase, source, target):
        copies = []
        for j in range(1, H):
            peer = lax.rem(h + j, H)
            copies.append(pltpu.make_async_remote_copy(
                src_ref=source(peer), dst_ref=target(j), send_sem=send_h.at[phase, j],
                recv_sem=recv_h.at[phase, j], device_id={"head": peer}, device_id_type=MESH))
        for copy in copies:
            copy.start()
        pending.extend(copies)
        return copies

    def head_gather(phase, buf):
        return head_send(phase, lambda peer: buf.at[h], lambda j: buf.at[h])

    def head_scatter(phase, out, into):
        return head_send(phase, lambda peer: out.at[peer], lambda j: into.at[j - 1])

    def seq_send(phase, source, target):
        copies = []
        for j in range(1, S):
            peer = lax.rem(s + j, S)
            copies.append(pltpu.make_async_remote_copy(
                src_ref=source(peer), dst_ref=target, send_sem=send_s.at[phase, j],
                recv_sem=recv_s.at[phase, j], device_id={"seq": peer}, device_id_type=MESH))
        for copy in copies:
            copy.start()
        pending.extend(copies)
        return copies

    def seq_gather(phase, buf):
        return seq_send(phase, lambda peer: buf.at[s], buf.at[s])

    def arrived(copies):
        for copy in copies:
            copy.wait_recv()

    def state_copy(phase, buf, slot, peer):
        return pltpu.make_async_remote_copy(
            src_ref=buf.at[slot], dst_ref=buf.at[slot], send_sem=send_s.at[phase, peer],
            recv_sem=recv_s.at[phase, slot], device_id={"seq": peer}, device_id_type=MESH)

    def wide(parts):
        return jnp.concatenate(parts, axis=1)

    def summed(own, into):
        total = own.astype(f32)
        for j in range(H - 1):
            total = total + into[j].astype(f32)
        return total

    xc[h, 0] = x_ref[...]
    xc[h, 1] = cot_ref[...]
    arrived(head_gather(0, xc))
    norm_gain = wide([ng_ref[p] for p in range(H)])
    ffn_gain = wide([fg_ref[p] for p in range(H)])
    xw = wide([xc[p, 0] for p in range(H)]).astype(f32)
    r1 = lax.rsqrt(jnp.mean(xw * xw, axis=1, keepdims=True) + EPS)
    n1 = xw * r1
    normed = (n1 * norm_gain).astype(bf16)
    cot_rows = wide([xc[p, 1] for p in range(H)])
    k = dot_nn(normed, wk_ref[...])
    v = dot_nn(normed, wv_ref[...])
    lowrank = dot_nn(normed, wr_ref[...])
    expand = we_ref[...].astype(f32)
    preact = fine(lowrank, expand, 1, 0) + gb_ref[...]
    logdecay = (jnp.minimum(preact, 0.0) - jnp.log1p(jnp.exp(-jnp.abs(preact)))) / 16.0
    ri = lax.broadcasted_iota(jnp.int32, (GROUP, GROUP), 0)
    ci = lax.broadcasted_iota(jnp.int32, (GROUP, GROUP), 1)
    lower = ri >= ci
    tri = lower.astype(f32)
    tri_up = (ri <= ci).astype(f32)

    def part(t, b):
        return t[b * GROUP : (b + 1) * GROUP]

    span = range(blocks)
    vb = [part(v, b) for b in span]
    cum = [fine(tri, part(logdecay, b), 1, 0) for b in span]
    last = [cum[b][GROUP - 1 : GROUP] for b in span]
    ef = [jnp.exp(last[b]) for b in span]
    kt = [part(k, b) * jnp.exp(last[b] - cum[b]) for b in span]
    ut = [fine(vb[b], kt[b], 0, 0) for b in span]
    state, total = ut[0], last[0]
    for b in range(1, blocks):
        state = state * ef[b] + ut[b]
        total = total + last[b]
    dts[s] = jnp.broadcast_to(total, (8, kw))
    stf[s] = state.astype(bf16)
    dt_copies = seq_gather(0, dts)
    for p in range(1, S):
        @pl.when(p > s)
        def _():
            state_copy(1, stf, s, p).start()

    q = dot_nn(normed, wq_ref[...]) * scale
    og = dot_nn(normed, wog_ref[...])
    eb = [jnp.exp(cum[b]) for b in span]
    en = [jnp.exp(-cum[b]) for b in span]
    qd = [part(q, b) * eb[b] for b in span]
    kd = [part(k, b) * en[b] for b in span]
    sc = [jnp.where(lower, fine(qd[b], kd[b], 1, 1), 0.0) for b in span]
    local = [fine(sc[b], vb[b], 1, 0) for b in span]
    for p in range(S):
        cs_a[p] = wide([normed[:, p * cb : (p + 1) * cb], cot_rows[:, p * cb : (p + 1) * cb]])
    cr_a[s] = cs_a[s]
    grad_hidden = cross_product(cot_rows, wd_ref[...])
    osig = jax.nn.sigmoid(og)
    swish = og * osig
    arrived(dt_copies)
    e_ref[...] = jnp.zeros_like(e_ref)
    for p in range(S - 1):
        @pl.when(p < s)
        def _():
            state_copy(1, stf, p, p).wait_recv()
            e_ref[...] = e_ref[...] * jnp.exp(dts[p, 0:1]) + stf[p].astype(f32)
    col_a = seq_send(2, lambda peer: cs_a.at[peer], cr_a.at[s])
    et = [e_ref[...]]
    for b in range(blocks - 1):
        et.append(et[b] * ef[b] + ut[b])
    mixed = jnp.concatenate([fine(qd[b], et[b], 1, 1) + local[b] for b in span], axis=0)
    rh = lax.rsqrt(jnp.mean(mixed * mixed, axis=1, keepdims=True) + HEAD_EPS)
    hn = mixed * rh
    branch = (hn * swish).astype(bf16)
    attn = dot_nn(branch, wo_ref[...])
    for p in range(H):
        rs_a[p] = attn[:, p * pw : (p + 1) * pw].astype(bf16)
    arrived(head_scatter(1, rs_a, rr_a))
    middle = x_ref[...].astype(f32) + summed(rs_a[h], rr_a)
    mid[h] = middle.astype(bf16)
    arrived(head_gather(2, mid))
    mw = wide([mid[p] for p in range(H)]).astype(f32)
    r2 = lax.rsqrt(jnp.mean(mw * mw, axis=1, keepdims=True) + EPS)
    n2 = mw * r2
    normed_two = (n2 * ffn_gain).astype(bf16)
    gate = dot_nn(normed_two, wg_ref[...])
    up = dot_nn(normed_two, wu_ref[...])
    gsig = jax.nn.sigmoid(gate)
    hidden = (gate * gsig * up).astype(bf16)
    grad_gate = (grad_hidden * up * gsig * (1.0 + gate * (1.0 - gsig))).astype(bf16)
    grad_up = (grad_hidden * gate * gsig).astype(bf16)
    gn2 = cross_product(grad_gate, wg_ref[...]) + cross_product(grad_up, wu_ref[...])
    ones = jnp.ones((8, full), f32)
    st_two[h] = fine(ones, gn2 * ffn_gain * n2, 1, 1)
    for p in range(H):
        rs_c[p] = gn2[:, p * pw : (p + 1) * pw].astype(bf16)
    c4 = head_scatter(3, rs_c, rr_c)
    c5 = head_gather(4, st_two)
    hid[s] = hidden
    ggu[s, 0] = grad_gate
    ggu[s, 1] = grad_up
    ffn = dot_nn(hidden, wd_ref[...])
    for p in range(H):
        rs_b[p] = ffn[:, p * pw : (p + 1) * pw].astype(bf16)
    arrived(c4)
    arrived(c5)
    grad_two = summed(rs_c[h], rr_c)
    stat = st_two[0]
    for p in range(1, H):
        stat = stat + st_two[p]
    n2_mine = mid[h].astype(f32) * r2
    grad_middle = cot_ref[...].astype(f32) + r2 * (
        grad_two * fg_ref[h] - n2_mine * (column_of(stat[0:1]) / full))
    gain_two = jnp.sum(grad_two * n2_mine, axis=0, keepdims=True)
    gbuf[h] = grad_middle.astype(bf16)
    c6 = head_gather(5, gbuf)
    c3 = head_scatter(6, rs_b, rr_b)
    arrived(c6)
    gbr = wide([gbuf[p] for p in range(H)])
    gbranch = cross_product(gbr, wo_ref[...])
    ghead = gbranch * swish
    gog = (gbranch * hn * osig * (1.0 + og * (1.0 - osig))).astype(bf16)
    gmix = rh * (ghead - hn * jnp.mean(ghead * hn, axis=1, keepdims=True))
    db = [part(gmix, b) for b in span]
    dtr = [fine(db[b], qd[b], 0, 0) for b in span]
    pull = dtr[blocks - 1]
    for b in reversed(range(blocks - 1)):
        pull = pull * ef[b] + dtr[b]
    stb[s] = pull.astype(bf16)
    for p in range(S - 1):
        @pl.when(p < s)
        def _():
            state_copy(3, stb, s, p).start()
    arrived(c3)
    out_ref[...] = (middle + summed(rs_b[h], rr_b)).astype(bf16)
    for p in range(S):
        cs_b[p] = wide([normed_two[:, p * cb : (p + 1) * cb], gbr[:, p * cb : (p + 1) * cb]])
    cr_b[s] = cs_b[s]
    pb = [jnp.where(lower, fine(db[b], vb[b], 1, 1), 0.0) for b in span]
    gqd = [fine(db[b], et[b], 1, 0) + fine(pb[b], kd[b], 1, 0) for b in span]
    gkd = [fine(pb[b], qd[b], 0, 0) for b in span]
    gv = [fine(sc[b], db[b], 0, 0) for b in span]
    g_ref[...] = jnp.zeros_like(g_ref)
    for p in reversed(range(1, S)):
        @pl.when(p > s)
        def _():
            state_copy(3, stb, p, p).wait_recv()
            g_ref[...] = g_ref[...] * jnp.exp(dts[p, 0:1]) + stb[p].astype(f32)
    hid_copies = seq_gather(4, hid)
    ggu_copies = seq_gather(5, ggu)
    col_b = seq_send(6, lambda peer: cs_b.at[peer], cr_b.at[s])
    gt = [None] * blocks
    gt[blocks - 1] = g_ref[...]
    for b in reversed(range(1, blocks)):
        gt[b - 1] = gt[b] * ef[b] + dtr[b]
    gkt = [fine(vb[b], gt[b], 1, 0) for b in span]
    gv = [gv[b] + fine(kt[b], gt[b], 1, 1) for b in span]
    tail = [kt[b] * gkt[b] for b in span]
    glog = [
        fine(tri_up, qd[b] * gqd[b] - kd[b] * gkd[b] - tail[b], 1, 0)
        + jnp.sum(tail[b], axis=0, keepdims=True)
        + ef[b] * jnp.sum(et[b] * gt[b], axis=0, keepdims=True)
        for b in span
    ]
    tall = lambda parts: jnp.concatenate(parts, axis=0)
    grad_query = (tall([gqd[b] * eb[b] for b in span]) * scale).astype(bf16)
    grad_keys = tall(
        [gkd[b] * en[b] + gkt[b] * jnp.exp(last[b] - cum[b]) for b in span]).astype(bf16)
    grad_values = tall(gv).astype(bf16)
    act[s] = wide([branch, grad_query, grad_keys, grad_values, gog])
    act_copies = seq_gather(7, act)
    grad_pre = tall(glog) / 16.0 * jax.nn.sigmoid(-preact)
    grad_expand = fine(lowrank, grad_pre, 0, 0)
    grad_bias = jnp.sum(grad_pre, axis=0, keepdims=True)
    glow = fine(grad_pre, expand, 1, 1)
    glow_t = fine(expand, grad_pre, 1, 1)
    gnormed = (
        cross_product(grad_query, wq_ref[...])
        + cross_product(grad_keys, wk_ref[...])
        + cross_product(grad_values, wv_ref[...])
        + cross_product(gog, wog_ref[...])
        + fine(glow, wr_ref[...].astype(f32), 1, 1)
    )
    rank = glow_t.shape[0]
    st_one[h, 0:8] = fine(ones, gnormed * norm_gain * n1, 1, 1)
    st_one[h, 8 : 8 + rank] = glow_t
    for p in range(H):
        rs_d[p] = gnormed[:, p * pw : (p + 1) * pw].astype(bf16)
    c7 = head_scatter(7, rs_d, rr_d)
    c8 = head_gather(8, st_one)
    arrived(c7)
    arrived(c8)
    grad_one = summed(rs_d[h], rr_d)
    small = st_one[0]
    for p in range(1, H):
        small = small + st_one[p]
    n1_mine = x_ref[...].astype(f32) * r1
    gin_ref[...] = grad_middle + r1 * (
        grad_one * ng_ref[h] - n1_mine * (column_of(small[0:1]) / full))
    gain_one = jnp.sum(grad_one * n1_mine, axis=0, keepdims=True)
    lanes = rows
    chunks = [grad_bias]
    for gain in (gain_one, gain_two):
        chunks += [gain[:, i * lanes : (i + 1) * lanes] for i in range(pw // lanes)]
    used = len(chunks)
    chunks.append(jnp.zeros((8 - used, lanes), f32))
    fsm[s, 0:rank] = grad_expand
    fsm[s, rank : rank + 8] = tall(chunks)
    fsm[s, rank + 8 : 2 * rank + 8] = small[8 : 8 + rank]
    fsm_copies = seq_gather(8, fsm)

    def tokens(t):
        return t.reshape(S * rows, t.shape[-1])

    arrived(col_a)
    cols_one = tokens(cr_a[...])
    arrived(hid_copies)
    gwd_ref[...] = rows_product(tokens(hid[...]), cols_one[:, cb:])
    arrived(ggu_copies)
    arrived(col_b)
    cols_two = tokens(cr_b[...])
    gwg_ref[...] = rows_product(cols_two[:, :cb], tokens(ggu[:, 0]))
    gwu_ref[...] = rows_product(cols_two[:, :cb], tokens(ggu[:, 1]))
    arrived(act_copies)
    gwo_ref[...] = rows_product(tokens(act[:, :, :vw]), tokens(cr_b[:, :, cb:]))
    mixes = rows_product(tokens(cr_a[:, :, :cb]), tokens(act[:, :, vw:]))
    gwq_ref[...] = mixes[:, :kw]
    gwk_ref[...] = mixes[:, kw : 2 * kw]
    gwv_ref[...] = mixes[:, 2 * kw : 2 * kw + vw]
    gwog_ref[...] = mixes[:, 2 * kw + vw :]
    arrived(fsm_copies)
    smalls = fsm[0]
    for p in range(1, S):
        smalls = smalls + fsm[p]
    gwe_ref[...] = smalls[:rank]
    gbias_ref[...] = smalls[rank : rank + 1]
    half = pw // lanes
    gng_ref[...] = wide([smalls[rank + 1 + i : rank + 2 + i] for i in range(half)])
    gfg_ref[...] = wide([smalls[rank + 1 + half + i : rank + 2 + half + i] for i in range(half)])
    acc = jnp.zeros((rank, cb), f32)
    for p in range(S):
        acc = acc + fine(fsm[p, rank + 8 : 2 * rank + 8], cr_a[p, :, :cb].astype(f32), 1, 0)
    gwr_ref[...] = acc
    for copy in pending:
        copy.wait_send()
    for p in range(S):
        @pl.when(p > s)
        def _():
            state_copy(1, stf, s, p).wait_send()

        @pl.when(p < s)
        def _():
            state_copy(3, stb, s, p).wait_send()


def kernel_body(block_input, norm_gain, w_query, w_key, w_value, w_outgate, w_rank, w_expand,
                gate_bias, w_output, ffn_gain, w_gate, w_up, w_down, cotangent):
    S, H = lax.axis_size("seq"), lax.axis_size("head")
    rows, pw = block_input.shape[1:]
    full = pw * H
    cb = full // S
    kw, vw, rank, ff = w_query.shape[1], w_value.shape[1], w_rank.shape[1], w_gate.shape[1]
    f32, bf16 = jnp.float32, jnp.bfloat16

    def shape(dims, dtype=f32):
        return jax.ShapeDtypeStruct(dims, dtype)

    outs = [shape((rows, pw), bf16), shape((rows, pw)), shape((1, pw)), shape((cb, kw)), shape((cb, kw)),
            shape((cb, vw)), shape((cb, vw)), shape((rank, cb)), shape((rank, kw)), shape((1, kw)),
            shape((vw, cb)), shape((1, pw)), shape((cb, ff)), shape((cb, ff)), shape((ff, cb))]

    def own(*dims, dtype=bf16):
        return pltpu.VMEM(dims, dtype)

    scratch = [
        own(H, 2, rows, pw), own(H, rows, pw), own(H - 1, rows, pw), own(H, rows, pw),
        own(H, rows, pw), own(H - 1, rows, pw), own(H, rows, pw), own(H - 1, rows, pw),
        own(H, 8, rows, dtype=f32), own(H, rows, pw), own(H, rows, pw), own(H - 1, rows, pw),
        own(H, 8 + rank, rows, dtype=f32), own(S, 8, kw, dtype=f32), own(S, vw, kw),
        own(S, vw, kw), own(vw, kw, dtype=f32), own(vw, kw, dtype=f32),
        own(S, rows, 2 * cb), own(S, rows, 2 * cb), own(S, rows, 2 * cb), own(S, rows, 2 * cb),
        own(S, rows, ff), own(S, 2, rows, ff), own(S, rows, 2 * kw + 3 * vw),
        own(S, 2 * rank + 8, rows, dtype=f32),
        pltpu.SemaphoreType.DMA((HEAD_PHASES + 1, H)), pltpu.SemaphoreType.DMA((HEAD_PHASES + 1, H)),
        pltpu.SemaphoreType.DMA((SEQ_PHASES, S)), pltpu.SemaphoreType.DMA((SEQ_PHASES, S)),
    ]
    got = pl.pallas_call(
        functools.partial(whole_kernel, S, H),
        out_shape=outs,
        in_specs=[pl.BlockSpec(memory_space=pltpu.VMEM)] * 15,
        out_specs=[pl.BlockSpec(memory_space=pltpu.VMEM)] * 15,
        scratch_shapes=scratch,
        compiler_params=pltpu.CompilerParams(
            collective_id=0, has_side_effects=True, vmem_limit_bytes=56 * 1024 * 1024),
    )(block_input.reshape(rows, pw), norm_gain.reshape(H, 1, pw), w_query, w_key, w_value, w_outgate,
      w_rank, w_expand, gate_bias.reshape(1, kw), w_output, ffn_gain.reshape(H, 1, pw), w_gate, w_up,
      w_down, cotangent.reshape(rows, pw))
    got = list(got)
    got[0] = got[0].reshape(1, rows, pw)
    got[1] = got[1].reshape(1, rows, pw)
    for i in (2, 9, 11):
        got[i] = got[i].reshape(-1)
    got[7] = got[7].T
    return tuple(got)


def solution(mesh):
    in_specs = (
        P(None, "seq", "head"),
        P(),
        P(None, "head"),
        P(None, "head"),
        P(None, "head"),
        P(None, "head"),
        P(),
        P(None, "head"),
        P("head"),
        P("head", None),
        P(),
        P(None, "head"),
        P(None, "head"),
        P("head", None),
        P(None, "seq", "head"),
    )
    out_specs = (
        P(None, "seq", "head"),
        P(None, "seq", "head"),
        P("head"),
        P("seq", "head"),
        P("seq", "head"),
        P("seq", "head"),
        P("seq", "head"),
        P("seq", None),
        P(None, "head"),
        P("head"),
        P("head", "seq"),
        P("head"),
        P("seq", "head"),
        P("seq", "head"),
        P("head", "seq"),
    )
    part = kernel_body if mesh.shape["seq"] <= 8 else body
    return jax.shard_map(part, mesh=mesh, in_specs=in_specs, out_specs=out_specs, check_vma=False)
```

```python
import functools

import jax
import jax.numpy as jnp
from jax import lax
from jax.experimental import pallas as pl
from jax.experimental.pallas import tpu as pltpu
from jax.sharding import PartitionSpec as P

MESH = pl.DeviceIdType.MESH

GROUP = 64


EPS = 1e-06
HEAD_EPS = 1e-05
PRECISE = lax.Precision.HIGHEST


def carried_in(shard, axis, combine, identity, reverse):
    peers, here = (lax.axis_size(axis), lax.axis_index(axis))
    everything = jax.tree.map(lambda part: lax.all_gather(part, axis), shard)
    start = jax.tree.map(
        lambda part, zero: jnp.broadcast_to(jnp.asarray(zero, part.dtype), part.shape),
        shard,
        identity,
    )

    def turn(k, before):
        at = peers - 1 - k if reverse else k
        reached = at > here if reverse else at < here
        new = combine(before, jax.tree.map(lambda part: part[at], everything))
        return jax.tree.map(lambda a, b: jnp.where(reached, a, b), new, before)

    return lax.fori_loop(0, peers, turn, start)


def matmul_high(left_side, right_side):
    return jnp.dot(left_side, right_side, precision=PRECISE)


def rows_product(left_side, right_side):
    return lax.dot_general(
        left_side, right_side, (((0,), (0,)), ((), ())), preferred_element_type=jnp.float32
    )


def cross_product(left_side, right_side):
    return lax.dot_general(
        left_side, right_side, (((1,), (1,)), ((), ())), preferred_element_type=jnp.float32
    )


def running_sum(tensor):
    length = tensor.shape[0]
    row_index = lax.broadcasted_iota(jnp.int32, (length, length), 0)
    col_index = lax.broadcasted_iota(jnp.int32, (length, length), 1)
    return matmul_high((row_index >= col_index).astype(jnp.float32), tensor)


def group_step(carry_state, block_inputs):
    q_block, k_block, v_block, g_block = block_inputs
    block_len = q_block.shape[0]
    cumulative = running_sum(g_block)
    final_sum = cumulative[-1]
    q_decay = q_block * jnp.exp(cumulative)
    k_decay = k_block * jnp.exp(-cumulative)
    scores = matmul_high(q_decay, k_decay.T)
    row_index = lax.broadcasted_iota(jnp.int32, (block_len, block_len), 0)
    col_index = lax.broadcasted_iota(jnp.int32, (block_len, block_len), 1)
    scores = jnp.where(row_index >= col_index, scores, jnp.zeros_like(scores))
    block_out = matmul_high(q_decay, carry_state) + matmul_high(scores, v_block)
    k_tail = k_block * jnp.exp(final_sum - cumulative)
    carry_state = jnp.exp(final_sum)[:, None] * carry_state + matmul_high(k_tail.T, v_block)
    return (carry_state, block_out)


def span_run(q_seq, k_seq, v_seq, g_seq, start_state):
    blocks = q_seq.shape[0] // GROUP

    def to_blocks(tensor):
        return tensor.reshape(blocks, GROUP, tensor.shape[-1])

    end_state, block_outs = lax.scan(
        jax.checkpoint(group_step),
        start_state,
        (to_blocks(q_seq), to_blocks(k_seq), to_blocks(v_seq), to_blocks(g_seq)),
    )
    return (block_outs.reshape(q_seq.shape[0], v_seq.shape[-1]), end_state)


def run_all(q_all, k_all, v_all, g_all, start_all):
    return jax.vmap(span_run)(q_all, k_all, v_all, g_all, start_all)


def combine(earlier, later):
    return (earlier[0] + later[0], jnp.exp(later[0])[:, :, None] * earlier[1] + later[1])


def body(
    block_input,
    norm_gain,
    w_query,
    w_key,
    w_value,
    w_outgate,
    w_rank,
    w_expand,
    gate_bias,
    w_output,
    ffn_gain,
    w_gate,
    w_up,
    w_down,
    cotangent,
):
    seq_count, span_len, part_width = block_input.shape
    row_count = seq_count * span_len
    head_count = lax.axis_size("head")
    full_width = part_width * head_count
    col_start = lax.axis_index("head") * part_width
    key_width = w_query.shape[1]
    value_width = w_value.shape[1]
    query_scale = key_width ** (-0.5)

    def per_seq(tensor):
        return tensor.reshape(seq_count, span_len, tensor.shape[-1])

    def mine(tensor):
        return lax.dynamic_slice_in_dim(tensor, col_start, part_width, tensor.ndim - 1)

    input_part = block_input.reshape(row_count, part_width)
    input_rows = lax.all_gather(input_part, "head", axis=1, tiled=True)
    input_wide = input_rows.astype(jnp.float32)
    inverse_one = lax.rsqrt(jnp.mean(input_wide * input_wide, axis=1, keepdims=True) + EPS)
    normal_one = input_wide * inverse_one
    normed = (normal_one * norm_gain).astype(jnp.bfloat16)
    query_proj = jnp.dot(normed, w_query, preferred_element_type=jnp.float32)
    key_proj = jnp.dot(normed, w_key, preferred_element_type=jnp.float32)
    value_proj = jnp.dot(normed, w_value, preferred_element_type=jnp.float32)
    outgate = jnp.dot(normed, w_outgate, preferred_element_type=jnp.float32)
    lowrank = jnp.dot(normed, w_rank, preferred_element_type=jnp.float32)
    expand_wide = w_expand.astype(jnp.float32)
    preact = matmul_high(lowrank, expand_wide) + gate_bias
    logdecay = jax.nn.log_sigmoid(preact) / 16.0
    q_seq = per_seq(query_proj) * query_scale
    k_seq = per_seq(key_proj)
    v_seq = per_seq(value_proj)
    g_seq = per_seq(logdecay)
    zero_state = jnp.zeros((seq_count, key_width, value_width), jnp.float32)
    local_out, local_state = run_all(q_seq, k_seq, v_seq, g_seq, zero_state)
    cumulative = jax.vmap(running_sum)(g_seq)
    carry_query = q_seq * jnp.exp(cumulative)
    decay_total = cumulative[:, -1, :]
    identity = (jnp.zeros_like(decay_total), zero_state)
    scanned = carried_in((decay_total, local_state), "seq", combine, identity, False)
    entering = scanned[1]
    mixer_out = local_out + jnp.einsum("sti,siv->stv", carry_query, entering, precision=PRECISE)
    mixer_out = mixer_out.reshape(row_count, value_width)
    head_inv = lax.rsqrt(jnp.mean(mixer_out * mixer_out, axis=1, keepdims=True) + HEAD_EPS)
    head_norm = mixer_out * head_inv
    outgate_sig = jax.nn.sigmoid(outgate)
    swish_gate = outgate * outgate_sig
    branch = (head_norm * swish_gate).astype(jnp.bfloat16)
    attn_part = jnp.dot(branch, w_output, preferred_element_type=jnp.float32)
    attn_mine = lax.psum_scatter(attn_part, "head", scatter_dimension=1, tiled=True)
    middle_part = input_part.astype(jnp.float32) + attn_mine
    middle_low = lax.all_gather(middle_part.astype(jnp.bfloat16), "head", axis=1, tiled=True)
    middle_wide = middle_low.astype(jnp.float32)
    inverse_two = lax.rsqrt(jnp.mean(middle_wide * middle_wide, axis=1, keepdims=True) + EPS)
    normal_two = middle_wide * inverse_two
    normed_two = (normal_two * ffn_gain).astype(jnp.bfloat16)
    gate_pre = jnp.dot(normed_two, w_gate, preferred_element_type=jnp.float32)
    up_pre = jnp.dot(normed_two, w_up, preferred_element_type=jnp.float32)
    gate_sig = jax.nn.sigmoid(gate_pre)
    hidden = (gate_pre * gate_sig * up_pre).astype(jnp.bfloat16)
    ffn_part = jnp.dot(hidden, w_down, preferred_element_type=jnp.float32)
    ffn_mine = lax.psum_scatter(
        ffn_part.astype(jnp.bfloat16), "head", scatter_dimension=1, tiled=True
    ).astype(jnp.float32)
    output = (middle_part + ffn_mine).astype(jnp.bfloat16).reshape(seq_count, span_len, part_width)
    grad_part = cotangent.reshape(row_count, part_width)
    grad_rows = lax.all_gather(grad_part, "head", axis=1, tiled=True)
    grad_hidden = cross_product(grad_rows, w_down)
    grad_gate = (grad_hidden * up_pre * gate_sig * (1.0 + gate_pre * (1.0 - gate_sig))).astype(
        jnp.bfloat16
    )
    grad_upper = (grad_hidden * gate_pre * gate_sig).astype(jnp.bfloat16)
    grad_normed_two = cross_product(grad_gate, w_gate) + cross_product(grad_upper, w_up)
    stat_part = jnp.sum(grad_normed_two * ffn_gain * normal_two, axis=1, keepdims=True)
    grad_two, stat_two = (
        lax.psum_scatter(grad_normed_two, "head", scatter_dimension=1, tiled=True),
        lax.psum_scatter(
            jnp.tile(stat_part, (1, head_count)), "head", scatter_dimension=1, tiled=True
        ),
    )
    normal_mine = mine(normal_two)
    grad_middle = grad_part.astype(jnp.float32) + inverse_two * (
        grad_two * mine(ffn_gain) - normal_mine * stat_two / full_width
    )
    gain_two = jnp.sum(grad_two * normal_mine, axis=0)
    grad_branch_rows = lax.all_gather(grad_middle.astype(jnp.bfloat16), "head", axis=1, tiled=True)
    grad_branch = cross_product(grad_branch_rows, w_output)
    grad_head = grad_branch * swish_gate
    grad_outgate = (
        grad_branch * head_norm * outgate_sig * (1.0 + outgate * (1.0 - outgate_sig))
    ).astype(jnp.bfloat16)
    grad_mixed = head_inv * (
        grad_head - head_norm * jnp.mean(grad_head * head_norm, axis=1, keepdims=True)
    )
    grad_seq = per_seq(grad_mixed)
    state_pull = jnp.einsum("sti,stv->siv", carry_query, grad_seq, precision=PRECISE)
    later = carried_in((decay_total, state_pull), "seq", combine, identity, True)
    later_grad = later[1]
    _, back_fn = jax.vjp(run_all, q_seq, k_seq, v_seq, g_seq, entering)
    grad_qseq, grad_kseq, grad_vseq, grad_gseq, _ = back_fn((grad_seq, later_grad))
    grad_query = (grad_qseq.reshape(row_count, key_width) * query_scale).astype(jnp.bfloat16)
    grad_keys = grad_kseq.reshape(row_count, key_width).astype(jnp.bfloat16)
    grad_values = grad_vseq.reshape(row_count, value_width).astype(jnp.bfloat16)
    grad_pre = grad_gseq.reshape(row_count, key_width) / 16.0 * jax.nn.sigmoid(-preact)
    grad_expand = lax.dot_general(lowrank, grad_pre, (((0,), (0,)), ((), ())), precision=PRECISE)
    grad_bias = jnp.sum(grad_pre, axis=0)
    grad_lowrank = lax.dot_general(
        grad_pre, expand_wide, (((1,), (1,)), ((), ())), precision=PRECISE
    )
    rank_wide = w_rank.astype(jnp.float32)
    grad_normed = (
        cross_product(grad_query, w_query)
        + cross_product(grad_keys, w_key)
        + cross_product(grad_values, w_value)
        + cross_product(grad_outgate, w_outgate)
        + lax.dot_general(grad_lowrank, rank_wide, (((1,), (1,)), ((), ())), precision=PRECISE)
    )
    stat_one_part = jnp.sum(grad_normed * norm_gain * normal_one, axis=1, keepdims=True)
    grad_one, stat_one, lowrank_total = (
        lax.psum_scatter(
            grad_normed.astype(jnp.bfloat16), "head", scatter_dimension=1, tiled=True
        ).astype(jnp.float32),
        lax.psum_scatter(
            jnp.tile(stat_one_part, (1, head_count)).astype(jnp.bfloat16),
            "head",
            scatter_dimension=1,
            tiled=True,
        ).astype(jnp.float32),
        lax.psum_scatter(
            jnp.tile(grad_lowrank, (1, head_count)).astype(jnp.bfloat16),
            "head",
            scatter_dimension=1,
            tiled=True,
        ).astype(jnp.float32),
    )
    normal_one_mine = mine(normal_one)
    grad_inputs = grad_middle + inverse_one * (
        grad_one * mine(norm_gain) - normal_one_mine * stat_one / full_width
    )
    gain_one = jnp.sum(grad_one * normal_one_mine, axis=0)
    def columns_of_all(tensor):
        return lax.all_to_all(tensor, "seq", split_axis=1, concat_axis=0, tiled=True)

    def tokens_of_all(tensor):
        return lax.all_gather(tensor, "seq", axis=0, tiled=True)

    columns_one = columns_of_all(normed)
    columns_two = columns_of_all(normed_two)
    columns_cot = columns_of_all(grad_rows)
    columns_branch = columns_of_all(grad_branch_rows)
    mixer_all = tokens_of_all(
        jnp.concatenate([grad_query, grad_keys, grad_values, grad_outgate], axis=1)
    )
    mixer_sum = rows_product(columns_one, mixer_all)
    wide = key_width
    grad_wout = rows_product(tokens_of_all(branch), columns_branch)
    grad_wgate = rows_product(columns_two, tokens_of_all(grad_gate))
    grad_wup = rows_product(columns_two, tokens_of_all(grad_upper))
    grad_wdown = rows_product(tokens_of_all(hidden), columns_cot)
    grad_wrank = rows_product(columns_one, tokens_of_all(lowrank_total.astype(jnp.bfloat16)))
    summed = (
        mixer_sum[:, :wide],
        mixer_sum[:, wide : 2 * wide],
        mixer_sum[:, 2 * wide : 2 * wide + value_width],
        mixer_sum[:, 2 * wide + value_width :],
        grad_wrank,
        grad_wout,
        grad_wgate,
        grad_wup,
        grad_wdown,
    )
    smalls = lax.psum((grad_expand, grad_bias, gain_one, gain_two), "seq")
    return (
        output,
        grad_inputs.reshape(seq_count, span_len, part_width),
        smalls[2],
        summed[0],
        summed[1],
        summed[2],
        summed[3],
        summed[4],
        smalls[0],
        smalls[1],
        summed[5],
        smalls[3],
        summed[6],
        summed[7],
        summed[8],
    )


def dot_nn(a, b):
    return lax.dot_general(a, b, (((1,), (0,)), ((), ())), preferred_element_type=jnp.float32)


def fine(a, b, left, right):
    return lax.dot_general(
        a,
        b,
        (((left,), (right,)), ((), ())),
        precision=PRECISE,
        preferred_element_type=jnp.float32,
    )


def column_of(row):
    size = row.shape[1]
    r = lax.broadcasted_iota(jnp.int32, (size, size), 0)
    c = lax.broadcasted_iota(jnp.int32, (size, size), 1)
    return jnp.sum(jnp.where(r == c, jnp.broadcast_to(row, (size, size)), 0.0), 1, keepdims=True)


HEAD_PHASES = 8
SEQ_PHASES = 9


def whole_kernel(S, H, *refs):
    (x_ref, ng_ref, wq_ref, wk_ref, wv_ref, wog_ref, wr_ref, we_ref, gb_ref, wo_ref, fg_ref,
     wg_ref, wu_ref, wd_ref, cot_ref) = refs[:15]
    (out_ref, gin_ref, gng_ref, gwq_ref, gwk_ref, gwv_ref, gwog_ref, gwr_ref, gwe_ref, gbias_ref,
     gwo_ref, gfg_ref, gwg_ref, gwu_ref, gwd_ref) = refs[15:30]
    (xc, rs_a, rr_a, mid, rs_b, rr_b, rs_c, rr_c, st_two, gbuf, rs_d, rr_d, st_one,
     dts, stf, stb, e_ref, g_ref, cs_a, cr_a, cs_b, cr_b, hid, ggu, act, fsm,
     send_h, recv_h, send_s, recv_s) = refs[30:]
    f32, bf16 = jnp.float32, jnp.bfloat16
    s, h = lax.axis_index("seq"), lax.axis_index("head")
    rows, pw = x_ref.shape
    full = pw * H
    cb = full // S
    kw, vw = wq_ref.shape[1], wv_ref.shape[1]
    blocks = rows // GROUP
    scale = kw ** (-0.5)
    pending = []

    barrier = pltpu.get_barrier_semaphore()
    for j in range(1, H):
        pl.semaphore_signal(barrier, inc=1, device_id={"head": lax.rem(h + j, H)}, device_id_type=MESH)
    for j in range(1, S):
        pl.semaphore_signal(barrier, inc=1, device_id={"seq": lax.rem(s + j, S)}, device_id_type=MESH)
    pl.semaphore_wait(barrier, H + S - 2)

    def head_send(phase, source, target):
        copies = []
        for j in range(1, H):
            peer = lax.rem(h + j, H)
            copies.append(pltpu.make_async_remote_copy(
                src_ref=source(peer), dst_ref=target(j), send_sem=send_h.at[phase, j],
                recv_sem=recv_h.at[phase, j], device_id={"head": peer}, device_id_type=MESH))
        for copy in copies:
            copy.start()
        pending.extend(copies)
        return copies

    def head_gather(phase, buf):
        return head_send(phase, lambda peer: buf.at[h], lambda j: buf.at[h])

    def head_scatter(phase, out, into):
        return head_send(phase, lambda peer: out.at[peer], lambda j: into.at[j - 1])

    def seq_send(phase, source, target):
        copies = []
        for j in range(1, S):
            peer = lax.rem(s + j, S)
            copies.append(pltpu.make_async_remote_copy(
                src_ref=source(peer), dst_ref=target, send_sem=send_s.at[phase, j],
                recv_sem=recv_s.at[phase, j], device_id={"seq": peer}, device_id_type=MESH))
        for copy in copies:
            copy.start()
        pending.extend(copies)
        return copies

    def seq_gather(phase, buf):
        return seq_send(phase, lambda peer: buf.at[s], buf.at[s])

    def arrived(copies):
        for copy in copies:
            copy.wait_recv()

    def state_copy(phase, buf, slot, peer):
        return pltpu.make_async_remote_copy(
            src_ref=buf.at[slot], dst_ref=buf.at[slot], send_sem=send_s.at[phase, peer],
            recv_sem=recv_s.at[phase, slot], device_id={"seq": peer}, device_id_type=MESH)

    def flip(t, n):
        return t + n - 2 * n * lax.rem(lax.div(t, n), 2)

    def relay(n, slots, first):
        copies = []
        for phase, buf in ((4, hid), (5, ggu)):
            for i, slot in enumerate(slots):
                copies.append(pltpu.make_async_remote_copy(
                    src_ref=buf.at[slot], dst_ref=buf.at[slot], send_sem=send_s.at[phase, first + i],
                    recv_sem=recv_s.at[phase, first + i], device_id={"seq": flip(s, n)},
                    device_id_type=MESH))
        for copy in copies:
            copy.start()
        pending.extend(copies)
        return copies

    def wide(parts):
        return jnp.concatenate(parts, axis=1)

    def summed(own, into):
        total = own.astype(f32)
        for j in range(H - 1):
            total = total + into[j].astype(f32)
        return total

    xc[h, 0] = x_ref[...]
    xc[h, 1] = cot_ref[...]
    arrived(head_gather(0, xc))
    norm_gain = wide([ng_ref[p] for p in range(H)])
    ffn_gain = wide([fg_ref[p] for p in range(H)])
    xw = wide([xc[p, 0] for p in range(H)]).astype(f32)
    r1 = lax.rsqrt(jnp.mean(xw * xw, axis=1, keepdims=True) + EPS)
    n1 = xw * r1
    normed = (n1 * norm_gain).astype(bf16)
    cot_rows = wide([xc[p, 1] for p in range(H)])
    k = dot_nn(normed, wk_ref[...])
    v = dot_nn(normed, wv_ref[...])
    lowrank = dot_nn(normed, wr_ref[...])
    expand = we_ref[...].astype(f32)
    preact = fine(lowrank, expand, 1, 0) + gb_ref[...]
    logdecay = (jnp.minimum(preact, 0.0) - jnp.log1p(jnp.exp(-jnp.abs(preact)))) / 16.0
    ri = lax.broadcasted_iota(jnp.int32, (GROUP, GROUP), 0)
    ci = lax.broadcasted_iota(jnp.int32, (GROUP, GROUP), 1)
    lower = ri >= ci
    tri = lower.astype(f32)
    tri_up = (ri <= ci).astype(f32)

    def part(t, b):
        return t[b * GROUP : (b + 1) * GROUP]

    span = range(blocks)
    vb = [part(v, b) for b in span]
    cum = [fine(tri, part(logdecay, b), 1, 0) for b in span]
    last = [cum[b][GROUP - 1 : GROUP] for b in span]
    ef = [jnp.exp(last[b]) for b in span]
    kt = [part(k, b) * jnp.exp(last[b] - cum[b]) for b in span]
    ut = [fine(vb[b], kt[b], 0, 0) for b in span]
    state, total = ut[0], last[0]
    for b in range(1, blocks):
        state = state * ef[b] + ut[b]
        total = total + last[b]
    dts[s] = jnp.broadcast_to(total, (8, kw))
    stf[s] = state.astype(bf16)
    dt_copies = seq_gather(0, dts)
    for p in range(1, S):
        @pl.when(p > s)
        def _():
            state_copy(1, stf, s, p).start()

    q = dot_nn(normed, wq_ref[...]) * scale
    og = dot_nn(normed, wog_ref[...])
    eb = [jnp.exp(cum[b]) for b in span]
    en = [jnp.exp(-cum[b]) for b in span]
    qd = [part(q, b) * eb[b] for b in span]
    kd = [part(k, b) * en[b] for b in span]
    sc = [jnp.where(lower, fine(qd[b], kd[b], 1, 1), 0.0) for b in span]
    local = [fine(sc[b], vb[b], 1, 0) for b in span]
    for p in range(S):
        cs_a[p] = wide([normed[:, p * cb : (p + 1) * cb], cot_rows[:, p * cb : (p + 1) * cb]])
    cr_a[s] = cs_a[s]
    grad_hidden = cross_product(cot_rows, wd_ref[...])
    osig = jax.nn.sigmoid(og)
    swish = og * osig
    arrived(dt_copies)
    e_ref[...] = jnp.zeros_like(e_ref)
    for p in range(S - 1):
        @pl.when(p < s)
        def _():
            state_copy(1, stf, p, p).wait_recv()
            e_ref[...] = e_ref[...] * jnp.exp(dts[p, 0:1]) + stf[p].astype(f32)
    col_a = seq_send(2, lambda peer: cs_a.at[peer], cr_a.at[s])
    et = [e_ref[...]]
    for b in range(blocks - 1):
        et.append(et[b] * ef[b] + ut[b])
    mixed = jnp.concatenate([fine(qd[b], et[b], 1, 1) + local[b] for b in span], axis=0)
    rh = lax.rsqrt(jnp.mean(mixed * mixed, axis=1, keepdims=True) + HEAD_EPS)
    hn = mixed * rh
    branch = (hn * swish).astype(bf16)
    attn = dot_nn(branch, wo_ref[...])
    for p in range(H):
        rs_a[p] = attn[:, p * pw : (p + 1) * pw].astype(bf16)
    arrived(head_scatter(1, rs_a, rr_a))
    middle = x_ref[...].astype(f32) + summed(rs_a[h], rr_a)
    mid[h] = middle.astype(bf16)
    arrived(head_gather(2, mid))
    mw = wide([mid[p] for p in range(H)]).astype(f32)
    r2 = lax.rsqrt(jnp.mean(mw * mw, axis=1, keepdims=True) + EPS)
    n2 = mw * r2
    normed_two = (n2 * ffn_gain).astype(bf16)
    gate = dot_nn(normed_two, wg_ref[...])
    up = dot_nn(normed_two, wu_ref[...])
    gsig = jax.nn.sigmoid(gate)
    hidden = (gate * gsig * up).astype(bf16)
    grad_gate = (grad_hidden * up * gsig * (1.0 + gate * (1.0 - gsig))).astype(bf16)
    grad_up = (grad_hidden * gate * gsig).astype(bf16)
    gn2 = cross_product(grad_gate, wg_ref[...]) + cross_product(grad_up, wu_ref[...])
    ones = jnp.ones((8, full), f32)
    st_two[h] = fine(ones, gn2 * ffn_gain * n2, 1, 1)
    for p in range(H):
        rs_c[p] = gn2[:, p * pw : (p + 1) * pw].astype(bf16)
    c4 = head_scatter(3, rs_c, rr_c)
    c5 = head_gather(4, st_two)
    hid[s] = hidden
    ggu[s, 0] = grad_gate
    ggu[s, 1] = grad_up
    relay_one = relay(4, [s], 1)
    ffn = dot_nn(hidden, wd_ref[...])
    for p in range(H):
        rs_b[p] = ffn[:, p * pw : (p + 1) * pw].astype(bf16)
    arrived(c4)
    arrived(c5)
    grad_two = summed(rs_c[h], rr_c)
    stat = st_two[0]
    for p in range(1, H):
        stat = stat + st_two[p]
    n2_mine = mid[h].astype(f32) * r2
    grad_middle = cot_ref[...].astype(f32) + r2 * (
        grad_two * fg_ref[h] - n2_mine * (column_of(stat[0:1]) / full))
    gain_two = jnp.sum(grad_two * n2_mine, axis=0, keepdims=True)
    gbuf[h] = grad_middle.astype(bf16)
    c6 = head_gather(5, gbuf)
    c3 = head_scatter(6, rs_b, rr_b)
    arrived(c6)
    gbr = wide([gbuf[p] for p in range(H)])
    gbranch = cross_product(gbr, wo_ref[...])
    ghead = gbranch * swish
    gog = (gbranch * hn * osig * (1.0 + og * (1.0 - osig))).astype(bf16)
    gmix = rh * (ghead - hn * jnp.mean(ghead * hn, axis=1, keepdims=True))
    db = [part(gmix, b) for b in span]
    dtr = [fine(db[b], qd[b], 0, 0) for b in span]
    pull = dtr[blocks - 1]
    for b in reversed(range(blocks - 1)):
        pull = pull * ef[b] + dtr[b]
    stb[s] = pull.astype(bf16)
    for p in range(S - 1):
        @pl.when(p < s)
        def _():
            state_copy(3, stb, s, p).start()
    arrived(relay_one)
    relay_two = relay(2, [s, flip(s, 4)], 2)
    arrived(c3)
    out_ref[...] = (middle + summed(rs_b[h], rr_b)).astype(bf16)
    for p in range(S):
        cs_b[p] = wide([normed_two[:, p * cb : (p + 1) * cb], gbr[:, p * cb : (p + 1) * cb]])
    cr_b[s] = cs_b[s]
    pb = [jnp.where(lower, fine(db[b], vb[b], 1, 1), 0.0) for b in span]
    gqd = [fine(db[b], et[b], 1, 0) + fine(pb[b], kd[b], 1, 0) for b in span]
    gkd = [fine(pb[b], qd[b], 0, 0) for b in span]
    gv = [fine(sc[b], db[b], 0, 0) for b in span]
    g_ref[...] = jnp.zeros_like(g_ref)
    for p in reversed(range(1, S)):
        @pl.when(p > s)
        def _():
            state_copy(3, stb, p, p).wait_recv()
            g_ref[...] = g_ref[...] * jnp.exp(dts[p, 0:1]) + stb[p].astype(f32)
    arrived(relay_two)
    relay_three = relay(1, [s, flip(s, 4), flip(s, 2), flip(flip(s, 2), 4)], 4)
    col_b = seq_send(6, lambda peer: cs_b.at[peer], cr_b.at[s])
    gt = [None] * blocks
    gt[blocks - 1] = g_ref[...]
    for b in reversed(range(1, blocks)):
        gt[b - 1] = gt[b] * ef[b] + dtr[b]
    gkt = [fine(vb[b], gt[b], 1, 0) for b in span]
    gv = [gv[b] + fine(kt[b], gt[b], 1, 1) for b in span]
    tail = [kt[b] * gkt[b] for b in span]
    glog = [
        fine(tri_up, qd[b] * gqd[b] - kd[b] * gkd[b] - tail[b], 1, 0)
        + jnp.sum(tail[b], axis=0, keepdims=True)
        + ef[b] * jnp.sum(et[b] * gt[b], axis=0, keepdims=True)
        for b in span
    ]
    tall = lambda parts: jnp.concatenate(parts, axis=0)
    grad_query = (tall([gqd[b] * eb[b] for b in span]) * scale).astype(bf16)
    grad_keys = tall(
        [gkd[b] * en[b] + gkt[b] * jnp.exp(last[b] - cum[b]) for b in span]).astype(bf16)
    grad_values = tall(gv).astype(bf16)
    act[s] = wide([branch, grad_query, grad_keys, grad_values, gog])
    act_copies = seq_gather(7, act)
    grad_pre = tall(glog) / 16.0 * jax.nn.sigmoid(-preact)
    grad_expand = fine(lowrank, grad_pre, 0, 0)
    grad_bias = jnp.sum(grad_pre, axis=0, keepdims=True)
    glow = fine(grad_pre, expand, 1, 1)
    glow_t = fine(expand, grad_pre, 1, 1)
    gnormed = (
        cross_product(grad_query, wq_ref[...])
        + cross_product(grad_keys, wk_ref[...])
        + cross_product(grad_values, wv_ref[...])
        + cross_product(gog, wog_ref[...])
        + fine(glow, wr_ref[...].astype(f32), 1, 1)
    )
    rank = glow_t.shape[0]
    st_one[h, 0:8] = fine(ones, gnormed * norm_gain * n1, 1, 1)
    st_one[h, 8 : 8 + rank] = glow_t
    for p in range(H):
        rs_d[p] = gnormed[:, p * pw : (p + 1) * pw].astype(bf16)
    c7 = head_scatter(7, rs_d, rr_d)
    c8 = head_gather(8, st_one)
    arrived(c7)
    arrived(c8)
    grad_one = summed(rs_d[h], rr_d)
    small = st_one[0]
    for p in range(1, H):
        small = small + st_one[p]
    n1_mine = x_ref[...].astype(f32) * r1
    gin_ref[...] = grad_middle + r1 * (
        grad_one * ng_ref[h] - n1_mine * (column_of(small[0:1]) / full))
    gain_one = jnp.sum(grad_one * n1_mine, axis=0, keepdims=True)
    lanes = rows
    chunks = [grad_bias]
    for gain in (gain_one, gain_two):
        chunks += [gain[:, i * lanes : (i + 1) * lanes] for i in range(pw // lanes)]
    used = len(chunks)
    chunks.append(jnp.zeros((8 - used, lanes), f32))
    fsm[s, 0:rank] = grad_expand
    fsm[s, rank : rank + 8] = tall(chunks)
    fsm[s, rank + 8 : 2 * rank + 8] = small[8 : 8 + rank]
    fsm_copies = seq_gather(8, fsm)

    def tokens(t):
        return t.reshape(S * rows, t.shape[-1])

    arrived(col_a)
    cols_one = tokens(cr_a[...])
    arrived(relay_three)
    gwd_ref[...] = rows_product(tokens(hid[...]), cols_one[:, cb:])
    arrived(col_b)
    cols_two = tokens(cr_b[...])
    gwg_ref[...] = rows_product(cols_two[:, :cb], tokens(ggu[:, 0]))
    gwu_ref[...] = rows_product(cols_two[:, :cb], tokens(ggu[:, 1]))
    arrived(act_copies)
    gwo_ref[...] = rows_product(tokens(act[:, :, :vw]), tokens(cr_b[:, :, cb:]))
    mixes = rows_product(tokens(cr_a[:, :, :cb]), tokens(act[:, :, vw:]))
    gwq_ref[...] = mixes[:, :kw]
    gwk_ref[...] = mixes[:, kw : 2 * kw]
    gwv_ref[...] = mixes[:, 2 * kw : 2 * kw + vw]
    gwog_ref[...] = mixes[:, 2 * kw + vw :]
    arrived(fsm_copies)
    smalls = fsm[0]
    for p in range(1, S):
        smalls = smalls + fsm[p]
    gwe_ref[...] = smalls[:rank]
    gbias_ref[...] = smalls[rank : rank + 1]
    half = pw // lanes
    gng_ref[...] = wide([smalls[rank + 1 + i : rank + 2 + i] for i in range(half)])
    gfg_ref[...] = wide([smalls[rank + 1 + half + i : rank + 2 + half + i] for i in range(half)])
    acc = jnp.zeros((rank, cb), f32)
    for p in range(S):
        acc = acc + fine(fsm[p, rank + 8 : 2 * rank + 8], cr_a[p, :, :cb].astype(f32), 1, 0)
    gwr_ref[...] = acc
    for copy in pending:
        copy.wait_send()
    for p in range(S):
        @pl.when(p > s)
        def _():
            state_copy(1, stf, s, p).wait_send()

        @pl.when(p < s)
        def _():
            state_copy(3, stb, s, p).wait_send()


def kernel_body(block_input, norm_gain, w_query, w_key, w_value, w_outgate, w_rank, w_expand,
                gate_bias, w_output, ffn_gain, w_gate, w_up, w_down, cotangent):
    S, H = lax.axis_size("seq"), lax.axis_size("head")
    rows, pw = block_input.shape[1:]
    full = pw * H
    cb = full // S
    kw, vw, rank, ff = w_query.shape[1], w_value.shape[1], w_rank.shape[1], w_gate.shape[1]
    f32, bf16 = jnp.float32, jnp.bfloat16

    def shape(dims, dtype=f32):
        return jax.ShapeDtypeStruct(dims, dtype)

    outs = [shape((rows, pw), bf16), shape((rows, pw)), shape((1, pw)), shape((cb, kw)), shape((cb, kw)),
            shape((cb, vw)), shape((cb, vw)), shape((rank, cb)), shape((rank, kw)), shape((1, kw)),
            shape((vw, cb)), shape((1, pw)), shape((cb, ff)), shape((cb, ff)), shape((ff, cb))]

    def own(*dims, dtype=bf16):
        return pltpu.VMEM(dims, dtype)

    scratch = [
        own(H, 2, rows, pw), own(H, rows, pw), own(H - 1, rows, pw), own(H, rows, pw),
        own(H, rows, pw), own(H - 1, rows, pw), own(H, rows, pw), own(H - 1, rows, pw),
        own(H, 8, rows, dtype=f32), own(H, rows, pw), own(H, rows, pw), own(H - 1, rows, pw),
        own(H, 8 + rank, rows, dtype=f32), own(S, 8, kw, dtype=f32), own(S, vw, kw),
        own(S, vw, kw), own(vw, kw, dtype=f32), own(vw, kw, dtype=f32),
        own(S, rows, 2 * cb), own(S, rows, 2 * cb), own(S, rows, 2 * cb), own(S, rows, 2 * cb),
        own(S, rows, ff), own(S, 2, rows, ff), own(S, rows, 2 * kw + 3 * vw),
        own(S, 2 * rank + 8, rows, dtype=f32),
        pltpu.SemaphoreType.DMA((HEAD_PHASES + 1, H)), pltpu.SemaphoreType.DMA((HEAD_PHASES + 1, H)),
        pltpu.SemaphoreType.DMA((SEQ_PHASES, S)), pltpu.SemaphoreType.DMA((SEQ_PHASES, S)),
    ]
    got = pl.pallas_call(
        functools.partial(whole_kernel, S, H),
        out_shape=outs,
        in_specs=[pl.BlockSpec(memory_space=pltpu.VMEM)] * 15,
        out_specs=[pl.BlockSpec(memory_space=pltpu.VMEM)] * 15,
        scratch_shapes=scratch,
        compiler_params=pltpu.CompilerParams(
            collective_id=0, has_side_effects=True, vmem_limit_bytes=56 * 1024 * 1024),
    )(block_input.reshape(rows, pw), norm_gain.reshape(H, 1, pw), w_query, w_key, w_value, w_outgate,
      w_rank, w_expand, gate_bias.reshape(1, kw), w_output, ffn_gain.reshape(H, 1, pw), w_gate, w_up,
      w_down, cotangent.reshape(rows, pw))
    got = list(got)
    got[0] = got[0].reshape(1, rows, pw)
    got[1] = got[1].reshape(1, rows, pw)
    for i in (2, 9, 11):
        got[i] = got[i].reshape(-1)
    got[7] = got[7].T
    return tuple(got)


def solution(mesh):
    in_specs = (
        P(None, "seq", "head"),
        P(),
        P(None, "head"),
        P(None, "head"),
        P(None, "head"),
        P(None, "head"),
        P(),
        P(None, "head"),
        P("head"),
        P("head", None),
        P(),
        P(None, "head"),
        P(None, "head"),
        P("head", None),
        P(None, "seq", "head"),
    )
    out_specs = (
        P(None, "seq", "head"),
        P(None, "seq", "head"),
        P("head"),
        P("seq", "head"),
        P("seq", "head"),
        P("seq", "head"),
        P("seq", "head"),
        P("seq", None),
        P(None, "head"),
        P("head"),
        P("head", "seq"),
        P("head"),
        P("seq", "head"),
        P("seq", "head"),
        P("head", "seq"),
    )
    part = kernel_body if mesh.shape["seq"] == 8 else body
    return jax.shard_map(part, mesh=mesh, in_specs=in_specs, out_specs=out_specs, check_vma=False)
```
